128 devices in a mesh: frame: 16 (over z_lo, y, core), space: 8 (over x, z_hi).
Axes of the slice: x: 4, y: 4, z: 4 (z_hi: 2, z_lo: 2; z = z_hi * 2 + z_lo), core: 2. Of those that a mesh axis runs over, the one named last changes fastest.
Arguments:
- q_spatial: bfloat16 [2, 16, 1536, 1152], P(None, 'frame', 'space'), may hold values from -220 to 220, as said below
- k_spatial: bfloat16 [2, 16, 1536, 1152], P(None, 'frame', 'space'), may hold values from -7 to 7, as said below
- v_spatial: bfloat16 [2, 16, 1536, 1152], P(None, 'frame', 'space'), may hold values from -6 to 6
- q_temporal: bfloat16 [2, 16, 1536, 1152], P(None, 'frame', 'space'), may hold values from -220 to 220, as said below
- k_temporal: bfloat16 [2, 16, 1536, 1152], P(None, 'frame', 'space'), may hold values from -7 to 7, as said below
- v_temporal: bfloat16 [2, 16, 1536, 1152], P(None, 'frame', 'space'), may hold values from -6 to 6
- grad_out: bfloat16 [2, 16, 1536, 1152], P(None, 'frame', 'space'), may hold values from -6 to 6
- inpaint_mask: int32 [2, 16, 1536], P(None, 'frame', 'space'), may hold values 0 or 1
- frame_order: int32 [16], replicated, may hold values from 0 to 15, each once
- rel_bias: float32 [16, 31], replicated, may hold values from -2 to 2
- w_qkv: bfloat16 [1152, 3456], replicated, may hold values from -0.1875 to 0.1875
- w_out: bfloat16 [1152, 1152], replicated, may hold values from -0.1875 to 0.1875
Outputs:
- grad_q_spatial: bfloat16 [2, 16, 1536, 1152], P(None, 'frame', 'space')
- grad_k_spatial: bfloat16 [2, 16, 1536, 1152], P(None, 'frame', 'space')
- grad_v_spatial: bfloat16 [2, 16, 1536, 1152], P(None, 'frame', 'space')
- grad_mid: bfloat16 [2, 16, 1536, 1152], P(None, 'frame', 'space')
The draws below stay inside these ranges and needn't reach their ends.
Inputs may be any that keep to these rules, and one draw needn't show every extreme that they name: `q_spatial`: bfloat16 values. `k_spatial`: bfloat16 values. `q_temporal`: bfloat16 values. `k_temporal`: bfloat16 values. `frame_order`: each time position once.
All inputs are finite; a program needn't handle non-finite values. No bound on the sum of `inpaint_mask` on one device may be relied on, other than what follows from the above.
Results may differ from the reference program's by a relative error of at most 0.012.
Values may be sent and summed in bfloat16 or wider, within the bound.
A program may use at most 256 MiB of HBM per device.

```python
import jax
import jax.numpy as jnp
from jax import lax

D = 1152
HEADS = 16
CLIPS = 2
FRAMES = 16
SEQ = 1536


def paired_rows(key, axis):
    shape = (CLIPS, FRAMES, SEQ, D)
    key = jax.random.fold_in(key, 100 + axis)
    base = jnp.clip(jax.random.normal(key, shape, jnp.float32), -6.0, 6.0)
    return base


def draw_q_spatial(key, part):
    base = paired_rows(key, 2)
    key = jax.random.fold_in(key, 3)
    fresh = jnp.clip(jax.random.normal(key, base.shape, jnp.float32), -6.0, 6.0)
    return fresh.astype(jnp.bfloat16)


def draw_k_spatial(key, part):
    base = paired_rows(key, 2)
    return base.astype(jnp.bfloat16)


def draw_q_temporal(key, part):
    base = paired_rows(key, 1)
    key = jax.random.fold_in(key, 7)
    fresh = jnp.clip(jax.random.normal(key, base.shape, jnp.float32), -6.0, 6.0)
    return fresh.astype(jnp.bfloat16)


def draw_k_temporal(key, part):
    base = paired_rows(key, 1)
    return base.astype(jnp.bfloat16)


def with_ends(array, rng, smallest, high):
    dims = array.shape
    index_at = [jax.random.randint(jax.random.fold_in(rng, axis), (), 0, dims[axis]) for axis in range(len(dims))]
    array = array.at[tuple(index_at)].set(smallest)
    longest = dims.index(max(dims))
    index_at[longest] = (index_at[longest] + 1) % dims[longest]
    return array.at[tuple(index_at)].set(high)


def shard_levels(key, shape, shards, least, top_value):
    factor_of, own = 1.0, jax.random.fold_in(key, 6)
    for position, shards_of in shards:
        steps = jnp.exp(jax.random.uniform(jax.random.fold_in(own, position), (shards_of,), jnp.float32, least / len(shards), top_value / len(shards)))
        factor_of = factor_of * jnp.repeat(steps, shape[position] // shards_of).reshape([-1 if axis == position else 1 for axis in range(len(shape))])
    return factor_of


def normal_values(own_key, shape, spread, limit, split=(), dtype=jnp.bfloat16):
    values = jax.random.normal(own_key, shape, jnp.float32) * spread
    if len(split) > 0:
        values = shard_levels(own_key, shape, split, -0.22, 0.18) * values
    return jnp.clip(values, min=-limit, max=limit).astype(dtype)


def setup_inputs(seed: int = 0) -> dict:
    splits = jax.random.split(jax.random.key(seed), 13)
    q_spatial = draw_q_spatial(jax.random.fold_in(splits[12], 71), 0)
    k_spatial = draw_k_spatial(jax.random.fold_in(splits[12], 71), 0)
    v_spatial = normal_values(splits[2], (CLIPS, FRAMES, SEQ, D), 1.0, 6.0, ((1, 16), (2, 8)))
    q_temporal = draw_q_temporal(jax.random.fold_in(splits[12], 71), 0)
    k_temporal = draw_k_temporal(jax.random.fold_in(splits[12], 71), 0)
    v_temporal = normal_values(splits[5], (CLIPS, FRAMES, SEQ, D), 1.0, 6.0, ((1, 16), (2, 8)))
    grad_out = normal_values(splits[6], (CLIPS, FRAMES, SEQ, D), 1.0, 6.0, ((1, 16), (2, 8)))
    inpaint_mask = with_ends((jax.random.randint(splits[7], (CLIPS, FRAMES, SEQ), 0, 2) < 1).astype(jnp.int32), jax.random.fold_in(splits[7], 1), 0, 1)
    frame_order = jax.random.permutation(splits[8], FRAMES).astype(jnp.int32)
    rel_bias = jnp.clip(jax.random.uniform(splits[9], (HEADS, 2 * FRAMES - 1), jnp.float32, -2.0, 2.0), -2.0, 2.0)
    w_qkv = normal_values(splits[10], (D, 3 * D), D ** -0.5, 0.1875)
    w_out = normal_values(splits[11], (D, D), D ** -0.5, 0.1875)
    return dict(q_spatial=q_spatial, k_spatial=k_spatial, v_spatial=v_spatial, q_temporal=q_temporal, k_temporal=k_temporal, v_temporal=v_temporal, grad_out=grad_out, inpaint_mask=inpaint_mask, frame_order=frame_order, rel_bias=rel_bias, w_qkv=w_qkv, w_out=w_out)


def attention_grads(queries, keys, values, cotangent, bias):
    scale = queries.shape[-1] ** -0.5
    q_full = queries.astype(jnp.float32)
    k_full = keys.astype(jnp.float32)
    v_full = values.astype(jnp.float32)
    c_full = cotangent.astype(jnp.float32)
    scores = jnp.einsum('bid,bjd->bij', q_full, k_full) * scale + bias
    scores = scores - jnp.max(scores, axis=-1, keepdims=True)
    weights = jnp.exp(scores)
    probs = weights / jnp.sum(weights, axis=-1, keepdims=True)
    probs_low = lax.optimization_barrier(probs.astype(jnp.bfloat16)).astype(jnp.float32)
    outputs = jnp.einsum('bij,bjd->bid', probs_low, v_full)
    delta = jnp.sum(c_full * outputs, axis=-1, keepdims=True)
    dprob = jnp.einsum('bid,bjd->bij', c_full, v_full)
    dscore = lax.optimization_barrier((probs * (dprob - delta) * scale).astype(jnp.bfloat16)).astype(jnp.float32)
    grad_q = jnp.einsum('bij,bjd->bid', dscore, k_full)
    grad_k = jnp.einsum('bij,bid->bjd', dscore, q_full)
    grad_v = jnp.einsum('bij,bid->bjd', probs_low, c_full)
    return grad_q.astype(jnp.bfloat16), grad_k.astype(jnp.bfloat16), grad_v.astype(jnp.bfloat16)


def reference(q_spatial, k_spatial, v_spatial, q_temporal, k_temporal, v_temporal, grad_out, inpaint_mask, frame_order, rel_bias, w_qkv, w_out):
    clips, frames, seq, width = q_spatial.shape
    head_dim = width // HEADS
    loss_cot = grad_out * inpaint_mask[..., None].astype(jnp.bfloat16)
    offsets = frame_order[:, None] - frame_order[None, :] + frames - 1
    table = lax.broadcasted_iota(jnp.int32, (frames, frames, 2 * frames - 1), 2)
    onehot = (offsets[:, :, None] == table).astype(jnp.float32)
    time_bias = jnp.sum(onehot[None] * rel_bias[:, None, None, :], axis=-1)

    def to_time(x):
        return x.reshape(clips, frames, seq, HEADS, head_dim).transpose(0, 2, 3, 1, 4).reshape(clips * seq * HEADS, frames, head_dim)

    def from_time(x):
        return x.reshape(clips, seq, HEADS, frames, head_dim).transpose(0, 3, 1, 2, 4).reshape(clips, frames, seq, width)

    bias_rows = jnp.broadcast_to(time_bias[None], (clips * seq, HEADS, frames, frames)).reshape(-1, frames, frames)
    t_grads = attention_grads(to_time(q_temporal), to_time(k_temporal), to_time(v_temporal), to_time(loss_cot), bias_rows)
    joined = jnp.concatenate([from_time(g) for g in t_grads], axis=-1).reshape(-1, 3 * width)
    grad_mid = jnp.dot(joined, w_qkv.T, preferred_element_type=jnp.float32).astype(jnp.bfloat16)
    s_cot = jnp.dot(grad_mid, w_out.T, preferred_element_type=jnp.float32).astype(jnp.bfloat16)
    s_cot = s_cot.reshape(clips, frames, seq, width)

    def one_frame(items):
        def to_heads(x):
            return x.reshape(seq, HEADS, head_dim).transpose(1, 0, 2)
        grads = attention_grads(to_heads(items[0]), to_heads(items[1]), to_heads(items[2]), to_heads(items[3]), jnp.float32(0.0))
        return tuple(g.transpose(1, 0, 2).reshape(seq, width) for g in grads)

    stacked = tuple(x.reshape(clips * frames, seq, width) for x in (q_spatial, k_spatial, v_spatial, s_cot))
    grad_q, grad_k, grad_v = lax.map(one_frame, stacked)
    shape = (clips, frames, seq, width)
    return grad_q.reshape(shape), grad_k.reshape(shape), grad_v.reshape(shape), grad_mid.reshape(shape)
```

```python
import functools

import jax
import jax.numpy as jnp
from jax import lax
from jax.experimental import pallas as pl
from jax.experimental.pallas import tpu as pltpu
from jax.sharding import PartitionSpec as P

HEADS = 16
E = 72
D = 1152
CLIPS = 2
FRAMES = 16
TOKENS = 192
SEQ = 1536
SPACE = 8
GROUPS = 3
ROWS = 128
BLOCK = 512
SCALE = E ** (-0.5)
LOG2E = 1.4426950408889634
MESH = pl.DeviceIdType.MESH
NN = (((1,), (0,)), ((), ()))
NT = (((1,), (1,)), ((), ()))
F32 = jnp.float32
BF16 = jnp.bfloat16


def dot(a, b, dims=NN):
    return lax.dot_general(a, b, dims, preferred_element_type=F32)


def softmax_grads(scores, dprob):
    weights = jnp.exp2(scores - jnp.max(scores, axis=1, keepdims=True))
    probs = weights * (1.0 / jnp.sum(weights, axis=1, keepdims=True))
    probs_low = probs.astype(BF16)
    delta = jnp.sum(probs_low.astype(F32) * dprob, axis=1, keepdims=True)
    return probs_low, (probs * ((dprob - delta) * SCALE)).astype(BF16)


def halves(low, high):
    lane = lax.broadcasted_iota(jnp.int32, low.shape, 1)
    return jnp.where(lane < 64, low, high)


def store_slabs(dst, main0, main1, third):
    for clip, main in enumerate((main0, main1)):
        by_head = main.reshape(SPACE, 2, E, 128)
        dst[:, clip, 0] = by_head[:, 0].astype(BF16)
        dst[:, clip, 1] = by_head[:, 1].astype(BF16)
    by_head = third.reshape(SPACE, 2, E, 128)
    even = by_head[:, 0].reshape(SPACE * E, 128)
    odd = by_head[:, 1].reshape(SPACE * E, 128)
    dst[:, 0, 2] = halves(even, pltpu.roll(odd, 64, 1)).reshape(SPACE, E, 128).astype(BF16)
    dst[:, 1, 2] = halves(pltpu.roll(even, 64, 1), odd).reshape(SPACE, E, 128).astype(BF16)


def temporal_kernel(
    qt, kt, vt, go, mask, fo_col, fo_row, rel_bias, qs, ks, vs, wqkv, wout,
    gm, recv,
    cot, tin, xg, bias, joined, gm_send, sin, send, wq, wo,
    t_send_sem, t_recv_sem, g_send_sem, g_recv_sem, s_send_sem, s_recv_sem, local_sem,
):
    mf, ms = lax.axis_index("frame"), lax.axis_index("space")
    loads = [
        pltpu.make_async_copy(src, dst, local_sem.at[n])
        for n, (src, dst) in enumerate(
            ((qs, sin.at[0]), (ks, sin.at[1]), (vs, sin.at[2]), (wqkv, wq), (wout, wo))
        )
    ]
    for copy in loads:
        copy.start()

    barrier = pltpu.get_barrier_semaphore()

    @pl.loop(1, FRAMES)
    def _(i):
        pl.semaphore_signal(barrier, inc=1, device_id=(lax.rem(mf + i, FRAMES), ms), device_id_type=MESH)

    @pl.loop(1, SPACE)
    def _(i):
        pl.semaphore_signal(barrier, inc=1, device_id=(mf, lax.rem(ms + i, SPACE)), device_id_type=MESH)

    pl.semaphore_wait(barrier, FRAMES + SPACE - 2)

    sources = (qt, kt, cot, vt)

    def t_copy(a, i):
        peer = lax.rem(mf + i, FRAMES)
        return pltpu.make_async_remote_copy(
            src_ref=sources[a].at[peer], dst_ref=tin.at[a, mf],
            send_sem=t_send_sem.at[a, i], recv_sem=t_recv_sem.at[a, i],
            device_id=(peer, ms), device_id_type=MESH,
        )

    def g_copy(i):
        peer = lax.rem(mf + i, FRAMES)
        return pltpu.make_async_remote_copy(
            src_ref=gm_send.at[peer], dst_ref=gm.at[mf],
            send_sem=g_send_sem.at[i], recv_sem=g_recv_sem.at[i],
            device_id=(peer, ms), device_id_type=MESH,
        )

    def s_copy(a, i):
        peer = lax.rem(ms + i, SPACE)
        return pltpu.make_async_remote_copy(
            src_ref=send.at[a, peer], dst_ref=recv.at[a, ms],
            send_sem=s_send_sem.at[a, i], recv_sem=s_recv_sem.at[a, i],
            device_id=(mf, peer), device_id_type=MESH,
        )

    def t_start(a):
        @pl.loop(1, FRAMES)
        def _(i):
            t_copy(a, i).start()

    t_start(0)
    t_start(1)
    cot[...] = (go[...].astype(F32) * mask[...].astype(F32)).astype(BF16)
    t_start(2)
    t_start(3)
    own = [
        pltpu.make_async_copy(sources[a].at[mf], tin.at[a, mf], local_sem.at[5 + a]) for a in range(4)
    ]
    for copy in own:
        copy.start()

    for a in range(3):
        loads[a].wait()

    @pl.loop(0, 3)
    def _(a):
        x = sin.at[a]
        main0 = x[0, 0:128, :].astype(F32).T
        main1 = x[1, 0:128, :].astype(F32).T
        third = jnp.concatenate([x[0, 128:192, :].astype(F32), x[1, 128:192, :].astype(F32)], axis=0).T
        store_slabs(send.at[a], main0, main1, third)
        for i in (2, 4, 6):
            s_copy(a, i).start()

    row = lax.broadcasted_iota(jnp.int32, (ROWS, ROWS), 0)
    col = lax.broadcasted_iota(jnp.int32, (ROWS, ROWS), 1)
    offset = jnp.where((row & 7) == (col & 7), fo_col[...] - fo_row[...] + (FRAMES - 1), -1)

    @pl.loop(0, HEADS)
    def _(h):
        total = jnp.full((ROWS, ROWS), -1e30, F32)
        for o in range(2 * FRAMES - 1):
            total = jnp.where(offset == o, rel_bias[h, o] * LOG2E, total)
        bias[h] = total

    for a in range(4):
        own[a].wait()

        @pl.loop(1, FRAMES)
        def _(i):
            t_copy(a, i).wait()

    @pl.loop(0, 3)
    def _(a):
        for i in (1, 7, 3, 5):
            s_copy(a, i).start()

    lane = lax.broadcasted_iota(jnp.int32, (1, 256), 1)

    @pl.loop(0, GROUPS)
    def _(g):
        for a in range(4):
            xg[a] = tin[a, :, g].astype(F32).reshape(ROWS, D).astype(BF16)
        carry = None
        for p in range(SPACE):
            window = slice(128 * p, 128 * p + 256)
            first = 16 * p
            m0 = jnp.where((lane >= first) & (lane < first + E), 1.0, 0.0).astype(BF16)
            m1 = jnp.where((lane >= first + E) & (lane < first + 2 * E), 1.0, 0.0).astype(BF16)

            def stacked(x):
                return jnp.concatenate([x * m0, x * m1], axis=0)

            q, k, c, v = (xg[a, :, window] for a in range(4))
            k2 = stacked(k)
            scores = dot(q, k2, NT)
            dprob = dot(c, stacked(v), NT)
            low, ds, low_t, ds_t = [], [], [], []
            for n in range(2):
                part = slice(128 * n, 128 * n + 128)
                pb, d = softmax_grads(scores[:, part] * (SCALE * LOG2E) + bias[2 * p + n], dprob[:, part])
                ds.append(d)
                low_t.append(pb.astype(F32).T.astype(BF16))
                ds_t.append(d.astype(F32).T.astype(BF16))
            outs = (
                dot(jnp.concatenate(ds, axis=1), k2),
                dot(jnp.concatenate(ds_t, axis=1), stacked(q)),
                dot(jnp.concatenate(low_t, axis=1), stacked(c)),
            )
            rows = pl.ds(pl.multiple_of(g * ROWS, ROWS), ROWS)
            for n, out in enumerate(outs):
                left = out[:, :128] if carry is None else out[:, :128] + carry[n]
                joined[rows, D * n + 128 * p:D * n + 128 * p + 128] = left.astype(BF16)
                if p == SPACE - 1:
                    joined[rows, D * n + 1024:D * n + D] = out[:, 128:].astype(BF16)
            carry = [out[:, 128:] for out in outs]

    loads[3].wait()
    mid = dot(joined[...], wq[...], NT)
    for g in range(GROUPS):
        gm_send[:, g] = mid[g * ROWS:(g + 1) * ROWS].reshape(FRAMES, 8, D).astype(BF16)

    @pl.loop(1, FRAMES)
    def _(i):
        g_copy(i).start()

    own_gm = pltpu.make_async_copy(gm_send.at[mf], gm.at[mf], local_sem.at[9])
    own_gm.start()
    own_gm.wait()

    @pl.loop(1, FRAMES)
    def _(i):
        g_copy(i).wait()

    loads[4].wait()
    mid = gm[...].astype(F32).reshape(CLIPS, TOKENS, D)
    mid = jnp.concatenate([mid[0, :128], mid[1, :128], mid[0, 128:], mid[1, 128:]], axis=0).astype(BF16)
    cot_t = dot(wo[...], mid, NT)
    store_slabs(send.at[3], cot_t[:, :128], cot_t[:, 128:256], cot_t[:, 256:])
    for i in (1, 7, 3, 5, 2, 4, 6):
        s_copy(3, i).start()
    own_s = [
        pltpu.make_async_copy(send.at[a, ms], recv.at[a, ms], local_sem.at[10 + a]) for a in range(4)
    ]
    for copy in own_s:
        copy.start()
    for copy in own_s:
        copy.wait()

    @pl.loop(0, 4)
    def _(a):
        @pl.loop(1, SPACE)
        def _(i):
            s_copy(a, i).wait()


def spatial_kernel(
    x, gq, gk, gv, q_t, k_t, v_t, c_t, q_n, c_n, sum_k, sum_v, thirds, send, recv,
    send_sem, recv_sem, local_sem,
):
    mf, ms = lax.axis_index("frame"), lax.axis_index("space")
    barrier = pltpu.get_barrier_semaphore()

    @pl.loop(1, SPACE)
    def _(i):
        pl.semaphore_signal(barrier, inc=1, device_id=(mf, lax.rem(ms + i, SPACE)), device_id_type=MESH)

    pl.semaphore_wait(barrier, SPACE - 1)

    def copy_of(a, i, clip, slab):
        peer = lax.rem(ms + i, SPACE)
        return pltpu.make_async_remote_copy(
            src_ref=send.at[a, peer, clip, slab], dst_ref=recv.at[a, ms, clip, slab],
            send_sem=send_sem.at[a, i, clip, slab], recv_sem=recv_sem.at[a, i, clip, slab],
            device_id=(mf, peer), device_id_type=MESH,
        )

    def start_slab(a, clip, slab):
        for i in (1, 7, 3, 5, 2, 4, 6):
            copy_of(a, i, clip, slab).start()

    def gather(a, clip, head, dst):
        for s in range(SPACE):
            dst[:, 128 * s:128 * s + 128] = x[a, s, clip, head]
        for m in range(SPACE // 2):
            low = x[a, 2 * m, clip, 2].astype(F32)
            high = x[a, 2 * m + 1, clip, 2].astype(F32)
            if head == 0:
                high = pltpu.roll(high, 64, 1)
            else:
                low = pltpu.roll(low, 64, 1)
            dst[:, 1024 + 128 * m:1152 + 128 * m] = halves(low, high).astype(BF16)

    def scatter(a, clip, head, tile, value):
        if tile < SPACE:
            send[a, tile, clip, head] = value.astype(BF16)
        elif head == 0:
            thirds[a, tile - SPACE] = value
        else:
            m = tile - SPACE
            other = thirds[a, m]
            send[a, 2 * m, clip, 2] = halves(other, pltpu.roll(value, 64, 1)).astype(BF16)
            send[a, 2 * m + 1, clip, 2] = halves(pltpu.roll(other, 64, 1), value).astype(BF16)

    @pl.loop(0, CLIPS)
    def _(clip):
        for head in range(2):
            for a, dst in enumerate((q_t, k_t, v_t, c_t)):
                gather(a, clip, head, dst)
            q_n[...] = q_t[...].astype(F32).T.astype(BF16)
            c_n[...] = c_t[...].astype(F32).T.astype(BF16)
            for b in range(SEQ // BLOCK):
                block = slice(b * BLOCK, (b + 1) * BLOCK)
                scores = dot(q_n[block], k_t[...]) * (SCALE * LOG2E)
                low, ds = softmax_grads(scores, dot(c_n[block], v_t[...]))
                to_q = dot(k_t[...], ds, NT)
                for n in range(BLOCK // 128):
                    scatter(0, clip, head, b * (BLOCK // 128) + n, to_q[:, 128 * n:128 * n + 128])
                to_k = dot(q_t[:, block], ds)
                to_v = dot(c_t[:, block], low)
                if b > 0:
                    to_k, to_v = sum_k[...] + to_k, sum_v[...] + to_v
                if b < SEQ // BLOCK - 1:
                    sum_k[...], sum_v[...] = to_k, to_v
            for n in range(SEQ // 128):
                scatter(1, clip, head, n, to_k[:, 128 * n:128 * n + 128])
                scatter(2, clip, head, n, to_v[:, 128 * n:128 * n + 128])
            for slab in (0,) if head == 0 else (1, 2):
                for a in range(3):
                    start_slab(a, clip, slab)

    for clip in range(CLIPS):
        own = [
            pltpu.make_async_copy(send.at[a, ms, clip], recv.at[a, ms, clip], local_sem.at[a])
            for a in range(3)
        ]
        for copy in own:
            copy.start()
        for a, out in enumerate((gq, gk, gv)):
            own[a].wait()

            @pl.loop(1, SPACE)
            def _(i):
                for slab in range(3):
                    copy_of(a, i, clip, slab).wait()

            main = recv[a, :, clip, 0:2].astype(F32).reshape(D, 128)
            out[clip, 0:128, :] = main.T.astype(BF16)
            third = recv[a, :, clip, 2].astype(F32)
            odd = pltpu.roll(third.reshape(SPACE * E, 128), 64, 1).reshape(SPACE, 1, E, 128)
            third = jnp.concatenate([third.reshape(SPACE, 1, E, 128), odd], axis=1).reshape(D, 128)
            out[clip, 128:192, :] = third.T[0:64].astype(BF16)


def on_device(
    q_spatial, k_spatial, v_spatial, q_temporal, k_temporal, v_temporal, grad_out,
    inpaint_mask, frame_order, rel_bias, w_qkv, w_out,
):
    chunks = (FRAMES, GROUPS, 8, D)
    hbm = pl.BlockSpec(memory_space=pl.ANY)
    vmem = pl.BlockSpec(memory_space=pltpu.VMEM)
    smem = pl.BlockSpec(memory_space=pltpu.SMEM)
    dma = pltpu.SemaphoreType.DMA
    slabs = (SPACE, CLIPS, 3, E, 128)
    times = jnp.repeat(frame_order, 8)
    mid, pieces = pl.pallas_call(
        temporal_kernel,
        out_shape=(jax.ShapeDtypeStruct(chunks, BF16), jax.ShapeDtypeStruct((4,) + slabs, BF16)),
        in_specs=[hbm, hbm, hbm, vmem, vmem, vmem, vmem, smem, hbm, hbm, hbm, hbm, hbm],
        out_specs=(vmem, hbm),
        scratch_shapes=[
            pltpu.VMEM(chunks, BF16),
            pltpu.VMEM((4,) + chunks, BF16),
            pltpu.VMEM((4, ROWS, D), BF16),
            pltpu.VMEM((HEADS, ROWS, ROWS), F32),
            pltpu.VMEM((GROUPS * ROWS, 3 * D), BF16),
            pltpu.VMEM(chunks, BF16),
            pltpu.VMEM((3, CLIPS, TOKENS, D), BF16),
            pltpu.VMEM((4,) + slabs, BF16),
            pltpu.VMEM((D, 3 * D), BF16),
            pltpu.VMEM((D, D), BF16),
            dma((4, FRAMES)), dma((4, FRAMES)), dma((FRAMES,)), dma((FRAMES,)),
            dma((4, SPACE)), dma((4, SPACE)), dma((14,)),
        ],
        compiler_params=pltpu.CompilerParams(
            collective_id=0, has_side_effects=True, vmem_limit_bytes=56 * 2**20
        ),
    )(
        q_temporal.reshape(chunks), k_temporal.reshape(chunks), v_temporal.reshape(chunks),
        grad_out.reshape(chunks), inpaint_mask.reshape(FRAMES, GROUPS, 8, 1),
        times.reshape(ROWS, 1), times.reshape(1, ROWS), rel_bias,
        q_spatial.reshape(CLIPS, TOKENS, D), k_spatial.reshape(CLIPS, TOKENS, D),
        v_spatial.reshape(CLIPS, TOKENS, D), w_qkv, w_out,
    )
    shape = (CLIPS, TOKENS, D)
    grads = pl.pallas_call(
        spatial_kernel,
        out_shape=(jax.ShapeDtypeStruct(shape, BF16),) * 3,
        in_specs=[vmem],
        out_specs=(vmem,) * 3,
        scratch_shapes=[
            *(pltpu.VMEM((E, SEQ), BF16) for _ in range(4)),
            *(pltpu.VMEM((SEQ, E), BF16) for _ in range(2)),
            *(pltpu.VMEM((E, SEQ), F32) for _ in range(2)),
            pltpu.VMEM((3, 4, E, 128), F32),
            pltpu.VMEM((3,) + slabs, BF16),
            pltpu.VMEM((3,) + slabs, BF16),
            dma((3, SPACE, CLIPS, 3)), dma((3, SPACE, CLIPS, 3)), dma((3,)),
        ],
        compiler_params=pltpu.CompilerParams(
            collective_id=1, has_side_effects=True, vmem_limit_bytes=56 * 2**20
        ),
    )(pieces)
    full = (CLIPS, 1, TOKENS, D)
    return (*(g.reshape(full) for g in grads), mid.reshape(full))


def solution(mesh):
    split = P(None, "frame", "space", None)
    in_specs = (split,) * 7 + (P(None, "frame", "space"), P(), P(), P(), P())
    return jax.shard_map(
        on_device, mesh=mesh, in_specs=in_specs, out_specs=(split,) * 4, check_vma=False
    )
```

```python
import jax
import jax.numpy as jnp
from jax import lax
from jax.experimental import pallas as pl
from jax.experimental.pallas import tpu as pltpu
from jax.sharding import PartitionSpec as P

HEADS = 16
E = 72
D = 1152
CLIPS = 2
FRAMES = 16
TOKENS = 192
SEQ = 1536
SPACE = 8
GROUPS = 3
ROWS = 128
BLOCK = 512
SCALE = E ** (-0.5)
LOG2E = 1.4426950408889634
MESH = pl.DeviceIdType.MESH
NN = (((1,), (0,)), ((), ()))
NT = (((1,), (1,)), ((), ()))
F32 = jnp.float32
BF16 = jnp.bfloat16


def dot(a, b, dims=NN):
    return lax.dot_general(a, b, dims, preferred_element_type=F32)


def softmax(scores):
    weights = jnp.exp2(scores - jnp.max(scores, axis=1, keepdims=True))
    return weights * (1.0 / jnp.sum(weights, axis=1, keepdims=True))


def score_grads(probs, probs_low, dprob):
    delta = jnp.sum(probs_low.astype(F32) * dprob, axis=1, keepdims=True)
    return (probs * (dprob - delta)).astype(BF16)


def halves(low, high):
    lane = lax.broadcasted_iota(jnp.int32, low.shape, 1)
    return jnp.where(lane < 64, low, high)


def store_slabs(dst, main0, main1, third):
    for clip, main in enumerate((main0, main1)):
        by_head = main.reshape(SPACE, 2, E, 128)
        dst[:, clip, 0] = by_head[:, 0].astype(BF16)
        dst[:, clip, 1] = by_head[:, 1].astype(BF16)
    by_head = third.reshape(SPACE, 2, E, 128)
    even = by_head[:, 0].reshape(SPACE * E, 128)
    odd = by_head[:, 1].reshape(SPACE * E, 128)
    dst[:, 0, 2] = halves(even, pltpu.roll(odd, 64, 1)).reshape(SPACE, E, 128).astype(BF16)
    dst[:, 1, 2] = halves(pltpu.roll(even, 64, 1), odd).reshape(SPACE, E, 128).astype(BF16)


def kernel(
    qt, kt, vt, go, mask, order, rel_bias, qs, ks, vs, wqkv, wout,
    gq, gk, gv, gm,
    cot, tin, xg, bias, joined, gm_send, gm_in, sin, send, recv, back, wq, wo,
    probs, q_t, k_t, v_t, c_t, row_n, sum_k, sum_v, thirds,
    t_send_sem, t_recv_sem, g_send_sem, g_recv_sem, s_send_sem, s_recv_sem, b_send_sem, b_recv_sem,
    local_sem, own_sem, out_sem,
):
    mf, ms = lax.axis_index("frame"), lax.axis_index("space")
    loads = [
        pltpu.make_async_copy(src, dst, local_sem.at[n])
        for n, (src, dst) in enumerate(
            ((go, sin.at[3]), (qs, sin.at[0]), (ks, sin.at[1]), (vs, sin.at[2]), (wqkv, wq), (wout, wo))
        )
    ]
    for copy in loads:
        copy.start()

    barrier = pltpu.get_barrier_semaphore()

    @pl.loop(1, FRAMES)
    def _(i):
        pl.semaphore_signal(barrier, inc=1, device_id=(lax.rem(mf + i, FRAMES), ms), device_id_type=MESH)

    @pl.loop(1, SPACE)
    def _(i):
        pl.semaphore_signal(barrier, inc=1, device_id=(mf, lax.rem(ms + i, SPACE)), device_id_type=MESH)

    pl.semaphore_wait(barrier, FRAMES + SPACE - 2)

    sources = (qt, kt, cot, vt)

    def t_copy(a, i):
        peer = lax.rem(mf + i, FRAMES)
        return pltpu.make_async_remote_copy(
            src_ref=sources[a].at[peer], dst_ref=tin.at[a, mf],
            send_sem=t_send_sem.at[a, i], recv_sem=t_recv_sem.at[a, i],
            device_id=(peer, ms), device_id_type=MESH,
        )

    def g_copy(i):
        peer = lax.rem(mf + i, FRAMES)
        return pltpu.make_async_remote_copy(
            src_ref=gm_send.at[peer], dst_ref=gm_in.at[mf],
            send_sem=g_send_sem.at[i], recv_sem=g_recv_sem.at[i],
            device_id=(peer, ms), device_id_type=MESH,
        )

    def s_copy(a, i, clip):
        peer = lax.rem(ms + i, SPACE)
        return pltpu.make_async_remote_copy(
            src_ref=send.at[a, peer, clip], dst_ref=recv.at[a, ms, clip],
            send_sem=s_send_sem.at[a, i, clip], recv_sem=s_recv_sem.at[a, i, clip],
            device_id=(mf, peer), device_id_type=MESH,
        )

    def own_copy(a, clip):
        return pltpu.make_async_copy(send.at[a, ms, clip], recv.at[a, ms, clip], own_sem.at[a, clip])

    def s_wait(a, clip):
        own_copy(a, clip).wait()

        @pl.loop(1, SPACE)
        def _(i):
            s_copy(a, i, clip).wait()

    def b_copy(a, i, clip, slab):
        peer = lax.rem(ms + i, SPACE)
        return pltpu.make_async_remote_copy(
            src_ref=send.at[a, peer, clip, slab], dst_ref=back.at[a, ms, clip, slab],
            send_sem=b_send_sem.at[a, i, clip, slab], recv_sem=b_recv_sem.at[a, i, clip, slab],
            device_id=(mf, peer), device_id_type=MESH,
        )

    def t_start(a):
        @pl.loop(1, FRAMES)
        def _(i):
            t_copy(a, i).start()

    t_start(0)
    t_start(1)
    loads[0].wait()
    row = lax.broadcasted_iota(jnp.int32, (TOKENS, TOKENS), 0)
    col = lax.broadcasted_iota(jnp.int32, (TOKENS, TOKENS), 1)
    for clip in range(CLIPS):
        diagonal = jnp.where(row == col, mask[clip].astype(F32), 0.0).astype(BF16)
        masked = dot(diagonal, sin[3, clip])
        cot[8 * clip:8 * clip + 8] = masked.reshape(8, GROUPS, 8, D).astype(BF16)
    t_start(2)
    t_start(3)
    own = [
        pltpu.make_async_copy(sources[a].at[mf], tin.at[a, mf], local_sem.at[6 + a]) for a in range(4)
    ]
    for copy in own:
        copy.start()

    for a in range(3):
        loads[1 + a].wait()

    @pl.loop(0, 3)
    def _(a):
        x = sin.at[a]
        main0 = x[0, 0:128, :].astype(F32).T
        main1 = x[1, 0:128, :].astype(F32).T
        third = jnp.concatenate([x[0, 128:192, :].astype(F32), x[1, 128:192, :].astype(F32)], axis=0).T
        store_slabs(send.at[a], main0, main1, third)
        for clip in range(CLIPS):
            own_copy(a, clip).start()
            for i in (2, 4, 6):
                s_copy(a, i, clip).start()

    row = lax.broadcasted_iota(jnp.int32, (ROWS, ROWS), 0)
    col = lax.broadcasted_iota(jnp.int32, (ROWS, ROWS), 1)
    offset = jnp.full((ROWS, ROWS), FRAMES - 1, jnp.int32)
    for f in range(FRAMES):
        offset = offset + jnp.where((row >> 3) == f, order[f], 0) - jnp.where((col >> 3) == f, order[f], 0)
    offset = jnp.where((row & 7) == (col & 7), offset, -1)

    @pl.loop(0, HEADS)
    def _(h):
        total = jnp.full((ROWS, ROWS), -1e30, F32)
        for o in range(2 * FRAMES - 1):
            total = jnp.where(offset == o, rel_bias[h, o] * LOG2E, total)
        bias[h] = total

    for a in range(4):
        own[a].wait()

        @pl.loop(1, FRAMES)
        def _(i):
            t_copy(a, i).wait()

    for a in range(2):
        for clip in range(CLIPS):
            for i in (1, 7, 3, 5):
                s_copy(a, i, clip).start()

    lane = lax.broadcasted_iota(jnp.int32, (1, 256), 1)

    @pl.loop(0, GROUPS)
    def _(g):
        for a in range(4):
            xg[a] = tin[a, :, g].astype(F32).reshape(ROWS, D).astype(BF16)
        carry = None
        for p in range(SPACE):
            window = slice(128 * p, 128 * p + 256)
            first = 16 * p
            m0 = jnp.where((lane >= first) & (lane < first + E), 1.0, 0.0).astype(BF16)
            m1 = jnp.where((lane >= first + E) & (lane < first + 2 * E), 1.0, 0.0).astype(BF16)

            def stacked(x):
                return jnp.concatenate([x * m0, x * m1], axis=0)

            q, k, c, v = (xg[a, :, window] for a in range(4))
            k2 = stacked(k)
            scores = dot(q, k2, NT)
            dprob = dot(c, stacked(v), NT)
            ds, low_t, ds_t = [], [], []
            for n in range(2):
                part = slice(128 * n, 128 * n + 128)
                pr = softmax(scores[:, part] * (SCALE * LOG2E) + bias[2 * p + n])
                low = pr.astype(BF16)
                d = score_grads(pr, low, dprob[:, part])
                ds.append(d)
                low_t.append(low.astype(F32).T.astype(BF16))
                ds_t.append(d.astype(F32).T.astype(BF16))
            outs = (
                dot(jnp.concatenate(ds, axis=1), k2) * SCALE,
                dot(jnp.concatenate(ds_t, axis=1), stacked(q)) * SCALE,
                dot(jnp.concatenate(low_t, axis=1), stacked(c)),
            )
            rows = pl.ds(pl.multiple_of(g * ROWS, ROWS), ROWS)
            for n, out in enumerate(outs):
                left = out[:, :128] if carry is None else out[:, :128] + carry[n]
                joined[rows, D * n + 128 * p:D * n + 128 * p + 128] = left.astype(BF16)
                if p == SPACE - 1:
                    joined[rows, D * n + 1024:D * n + D] = out[:, 128:].astype(BF16)
            carry = [out[:, 128:] for out in outs]

    loads[4].wait()
    mid = dot(joined[...], wq[...], NT)
    for g in range(GROUPS):
        gm_send[:, g] = mid[g * ROWS:(g + 1) * ROWS].reshape(FRAMES, 8, D).astype(BF16)

    @pl.loop(1, FRAMES)
    def _(i):
        g_copy(i).start()

    own_gm = pltpu.make_async_copy(gm_send.at[mf], gm_in.at[mf], local_sem.at[10])
    own_gm.start()
    for i in (1, 7, 3, 5):
        s_copy(2, i, 0).start()
    own_gm.wait()

    @pl.loop(1, FRAMES)
    def _(i):
        g_copy(i).wait()

    gm_out = pltpu.make_async_copy(gm_in, gm, local_sem.at[11])
    gm_out.start()
    loads[5].wait()
    mid = gm_in[...].astype(F32).reshape(CLIPS, TOKENS, D)
    mid = jnp.concatenate([mid[0, :128], mid[1, :128], mid[0, 128:], mid[1, 128:]], axis=0).astype(BF16)
    cot_t = dot(wo[...], mid, NT)
    store_slabs(send.at[3], cot_t[:, :128], cot_t[:, 128:256], cot_t[:, 256:])
    for clip in range(CLIPS):
        if clip == 1:
            for i in (1, 7, 3, 5):
                s_copy(2, i, 1).start()
        own_copy(3, clip).start()
        for i in (1, 7, 3, 5, 2, 4, 6):
            s_copy(3, i, clip).start()

    def gather(a, clip, head, dst):
        for s in range(SPACE):
            dst[:, 128 * s:128 * s + 128] = recv[a, s, clip, head]
        for m in range(SPACE // 2):
            low = recv[a, 2 * m, clip, 2].astype(F32)
            high = recv[a, 2 * m + 1, clip, 2].astype(F32)
            if head == 0:
                high = pltpu.roll(high, 64, 1)
            else:
                low = pltpu.roll(low, 64, 1)
            dst[:, 1024 + 128 * m:1152 + 128 * m] = halves(low, high).astype(BF16)

    @pl.loop(0, CLIPS)
    def _(clip):
        s_wait(0, clip)
        s_wait(1, clip)
        for head in range(2):
            gather(0, clip, head, q_t)
            gather(1, clip, head, k_t)
            row_n[...] = q_t[...].astype(F32).T.astype(BF16)
            for b in range(SEQ // BLOCK):
                block = slice(b * BLOCK, (b + 1) * BLOCK)
                scores = dot(row_n[block], k_t[...]) * (SCALE * LOG2E)
                probs[2 * clip + head, block] = softmax(scores).astype(BF16)

    def scatter(a, clip, head, tile, value):
        if tile < SPACE:
            send[a, tile, clip, head] = value.astype(BF16)
        elif head == 0:
            thirds[a, tile - SPACE] = value
        else:
            m = tile - SPACE
            other = thirds[a, m]
            send[a, 2 * m, clip, 2] = halves(other, pltpu.roll(value, 64, 1)).astype(BF16)
            send[a, 2 * m + 1, clip, 2] = halves(pltpu.roll(other, 64, 1), value).astype(BF16)

    @pl.loop(0, CLIPS)
    def _(clip):
        s_wait(2, clip)
        s_wait(3, clip)
        for head in range(2):
            for a, dst in enumerate((q_t, k_t, v_t, c_t)):
                gather(a, clip, head, dst)
            row_n[...] = c_t[...].astype(F32).T.astype(BF16)
            for b in range(SEQ // BLOCK):
                block = slice(b * BLOCK, (b + 1) * BLOCK)
                low = probs[2 * clip + head, block]
                ds = score_grads(low.astype(F32), low, dot(row_n[block], v_t[...]))
                to_q = dot(k_t[...], ds, NT) * SCALE
                for n in range(BLOCK // 128):
                    scatter(0, clip, head, b * (BLOCK // 128) + n, to_q[:, 128 * n:128 * n + 128])
                to_k = dot(q_t[:, block], ds)
                to_v = dot(c_t[:, block], low)
                if b > 0:
                    to_k, to_v = sum_k[...] + to_k, sum_v[...] + to_v
                if b < SEQ // BLOCK - 1:
                    sum_k[...], sum_v[...] = to_k, to_v
            to_k = to_k * SCALE
            for n in range(SEQ // 128):
                scatter(1, clip, head, n, to_k[:, 128 * n:128 * n + 128])
                scatter(2, clip, head, n, to_v[:, 128 * n:128 * n + 128])
            for slab in (0,) if head == 0 else (1, 2):
                for a in range(3):
                    for i in (1, 7, 3, 5, 2, 4, 6):
                        b_copy(a, i, clip, slab).start()

    outs = []
    for clip in range(CLIPS):
        own = [
            pltpu.make_async_copy(send.at[a, ms, clip], back.at[a, ms, clip], local_sem.at[a])
            for a in range(3)
        ]
        for copy in own:
            copy.start()
        for a, out in enumerate((gq, gk, gv)):
            own[a].wait()

            @pl.loop(1, SPACE)
            def _(i):
                for slab in range(3):
                    b_copy(a, i, clip, slab).wait()

            main = back[a, :, clip, 0:2].astype(F32).reshape(D, 128)
            sin[a, clip, 0:128, :] = main.T.astype(BF16)
            third = back[a, :, clip, 2].astype(F32)
            odd = pltpu.roll(third.reshape(SPACE * E, 128), 64, 1).reshape(SPACE, 1, E, 128)
            third = jnp.concatenate([third.reshape(SPACE, 1, E, 128), odd], axis=1).reshape(D, 128)
            sin[a, clip, 128:192, :] = third.T[0:64].astype(BF16)
            outs.append(pltpu.make_async_copy(sin.at[a, clip], out.at[clip], out_sem.at[a, clip]))
            outs[-1].start()
    gm_out.wait()
    for copy in outs:
        copy.wait()


def copy_kernel(a, b, c, d, a_out, b_out, c_out, d_out, sem):
    copies = []
    for n, (src, dst) in enumerate(((a, a_out), (b, b_out), (c, c_out), (d, d_out))):
        for part in range(4):
            rows = pl.ds(96 * part, 96)
            copies.append(pltpu.make_async_copy(src.at[rows], dst.at[rows], sem.at[n, part]))
            copies[-1].start()
    for copy in copies:
        copy.wait()


def on_device(
    q_spatial, k_spatial, v_spatial, q_temporal, k_temporal, v_temporal, grad_out,
    inpaint_mask, frame_order, rel_bias, w_qkv, w_out,
):
    chunks = (FRAMES, GROUPS, 8, D)
    shape = (CLIPS, TOKENS, D)
    slabs = (SPACE, CLIPS, 3, E, 128)
    hbm = pl.BlockSpec(memory_space=pl.ANY)
    vmem = pl.BlockSpec(memory_space=pltpu.VMEM)
    smem = pl.BlockSpec(memory_space=pltpu.SMEM)
    dma = pltpu.SemaphoreType.DMA
    results = pl.pallas_call(
        kernel,
        out_shape=(jax.ShapeDtypeStruct(shape, BF16),) * 3 + (jax.ShapeDtypeStruct(chunks, BF16),),
        in_specs=[hbm, hbm, hbm, hbm, vmem, smem, smem, hbm, hbm, hbm, hbm, hbm],
        out_specs=(hbm,) * 4,
        scratch_shapes=[
            pltpu.VMEM(chunks, BF16),
            pltpu.VMEM((4,) + chunks, BF16),
            pltpu.VMEM((4, ROWS, D), BF16),
            pltpu.VMEM((HEADS, ROWS, ROWS), F32),
            pltpu.VMEM((GROUPS * ROWS, 3 * D), BF16),
            pltpu.VMEM(chunks, BF16),
            pltpu.VMEM(chunks, BF16),
            pltpu.VMEM((4,) + shape, BF16),
            pltpu.VMEM((4,) + slabs, BF16),
            pltpu.VMEM((4,) + slabs, BF16),
            pltpu.VMEM((3,) + slabs, BF16),
            pltpu.VMEM((D, 3 * D), BF16),
            pltpu.VMEM((D, D), BF16),
            pltpu.VMEM((4, SEQ, SEQ), BF16),
            *(pltpu.VMEM((E, SEQ), BF16) for _ in range(4)),
            pltpu.VMEM((SEQ, E), BF16),
            *(pltpu.VMEM((E, SEQ), F32) for _ in range(2)),
            pltpu.VMEM((3, 4, E, 128), F32),
            dma((4, FRAMES)), dma((4, FRAMES)), dma((FRAMES,)), dma((FRAMES,)),
            dma((4, SPACE, CLIPS)), dma((4, SPACE, CLIPS)),
            dma((3, SPACE, CLIPS, 3)), dma((3, SPACE, CLIPS, 3)),
            dma((12,)), dma((4, CLIPS)), dma((3, CLIPS)),
        ],
        compiler_params=pltpu.CompilerParams(
            collective_id=0, has_side_effects=True, vmem_limit_bytes=63 * 2**20
        ),
    )(
        q_temporal.reshape(chunks), k_temporal.reshape(chunks), v_temporal.reshape(chunks),
        grad_out.reshape(shape), inpaint_mask, frame_order, rel_bias,
        q_spatial.reshape(shape), k_spatial.reshape(shape), v_spatial.reshape(shape), w_qkv, w_out,
    )
    flat = (CLIPS * TOKENS, D)
    results = pl.pallas_call(
        copy_kernel,
        out_shape=(jax.ShapeDtypeStruct(flat, BF16),) * 4,
        in_specs=[hbm] * 4,
        out_specs=(hbm,) * 4,
        scratch_shapes=[dma((4, 4))],
    )(*(r.reshape(flat) for r in results))
    return tuple(r.reshape(CLIPS, 1, TOKENS, D) for r in results)


def solution(mesh):
    split = P(None, "frame", "space", None)
    in_specs = (split,) * 7 + (P(None, "frame", "space"), P(), P(), P(), P())
    return jax.shard_map(
        on_device, mesh=mesh, in_specs=in_specs, out_specs=(split,) * 4, check_vma=False
    )
```

```python
import jax
import jax.numpy as jnp
from jax import lax
from jax.experimental import pallas as pl
from jax.experimental.pallas import tpu as pltpu
from jax.sharding import PartitionSpec as P

HEADS = 16
E = 72
D = 1152
CLIPS = 2
FRAMES = 16
TOKENS = 192
SEQ = 1536
SPACE = 8
GROUPS = 3
ROWS = 128
BLOCK = 512
SCALE = E ** (-0.5)
LOG2E = 1.4426950408889634
MESH = pl.DeviceIdType.MESH
NN = (((1,), (0,)), ((), ()))
NT = (((1,), (1,)), ((), ()))
F32 = jnp.float32
BF16 = jnp.bfloat16


def dot(a, b, dims=NN):
    return lax.dot_general(a, b, dims, preferred_element_type=F32)


def softmax(scores):
    weights = jnp.exp2(scores - jnp.max(scores, axis=1, keepdims=True))
    return weights * (1.0 / jnp.sum(weights, axis=1, keepdims=True))


def score_grads(probs, probs_low, dprob):
    delta = jnp.sum(probs_low.astype(F32) * dprob, axis=1, keepdims=True)
    return (probs * (dprob - delta)).astype(BF16)


def halves(low, high):
    lane = lax.broadcasted_iota(jnp.int32, low.shape, 1)
    return jnp.where(lane < 64, low, high)


def store_slabs(dst, main0, main1, third):
    for clip, main in enumerate((main0, main1)):
        by_head = main.reshape(SPACE, 2, E, 128)
        dst[:, clip, 0] = by_head[:, 0].astype(BF16)
        dst[:, clip, 1] = by_head[:, 1].astype(BF16)
    by_head = third.reshape(SPACE, 2, E, 128)
    even = by_head[:, 0].reshape(SPACE * E, 128)
    odd = by_head[:, 1].reshape(SPACE * E, 128)
    dst[:, 0, 2] = halves(even, pltpu.roll(odd, 64, 1)).reshape(SPACE, E, 128).astype(BF16)
    dst[:, 1, 2] = halves(pltpu.roll(even, 64, 1), odd).reshape(SPACE, E, 128).astype(BF16)


def kernel(
    qt, kt, vt, go, mask, order, rel_bias, qs, ks, vs, wqkv, wout,
    gq, gk, gv, gm,
    cot, tin, xg, bias, joined, gm_send, gm_in, sin, send, recv, back, wq, wo,
    probs, q_t, k_t, v_t, c_t, row_n, sum_k, sum_v, thirds,
    t_send_sem, t_recv_sem, g_send_sem, g_recv_sem, s_send_sem, s_recv_sem, b_send_sem, b_recv_sem,
    local_sem, own_sem, out_sem,
):
    mf, ms = lax.axis_index("frame"), lax.axis_index("space")
    loads = [
        pltpu.make_async_copy(src, dst, local_sem.at[n])
        for n, (src, dst) in enumerate(
            ((go, sin.at[3]), (qs, sin.at[0]), (ks, sin.at[1]), (vs, sin.at[2]), (wqkv, wq), (wout, wo))
        )
    ]
    for copy in loads:
        copy.start()

    barrier = pltpu.get_barrier_semaphore()

    @pl.loop(1, FRAMES)
    def _(i):
        pl.semaphore_signal(barrier, inc=1, device_id=(lax.rem(mf + i, FRAMES), ms), device_id_type=MESH)

    @pl.loop(1, SPACE)
    def _(i):
        pl.semaphore_signal(barrier, inc=1, device_id=(mf, lax.rem(ms + i, SPACE)), device_id_type=MESH)

    pl.semaphore_wait(barrier, FRAMES + SPACE - 2)

    sources = (qt, kt, cot, vt)

    def t_copy(a, i):
        peer = lax.rem(mf + i, FRAMES)
        return pltpu.make_async_remote_copy(
            src_ref=sources[a].at[peer], dst_ref=tin.at[a, mf],
            send_sem=t_send_sem.at[a, i], recv_sem=t_recv_sem.at[a, i],
            device_id=(peer, ms), device_id_type=MESH,
        )

    def g_copy(i):
        peer = lax.rem(mf + i, FRAMES)
        return pltpu.make_async_remote_copy(
            src_ref=gm_send.at[peer], dst_ref=gm_in.at[mf],
            send_sem=g_send_sem.at[i], recv_sem=g_recv_sem.at[i],
            device_id=(peer, ms), device_id_type=MESH,
        )

    def s_copy(a, i, clip):
        peer = lax.rem(ms + i, SPACE)
        return pltpu.make_async_remote_copy(
            src_ref=send.at[a, peer, clip], dst_ref=recv.at[a, ms, clip],
            send_sem=s_send_sem.at[a, i, clip], recv_sem=s_recv_sem.at[a, i, clip],
            device_id=(mf, peer), device_id_type=MESH,
        )

    def own_copy(a, clip):
        return pltpu.make_async_copy(send.at[a, ms, clip], recv.at[a, ms, clip], own_sem.at[a, clip])

    def s_wait(a, clip):
        own_copy(a, clip).wait()

        @pl.loop(1, SPACE)
        def _(i):
            s_copy(a, i, clip).wait()

    def b_copy(a, i, clip, slab):
        peer = lax.rem(ms + i, SPACE)
        return pltpu.make_async_remote_copy(
            src_ref=send.at[a, peer, clip, slab], dst_ref=back.at[a, ms, clip, slab],
            send_sem=b_send_sem.at[a, i, clip, slab], recv_sem=b_recv_sem.at[a, i, clip, slab],
            device_id=(mf, peer), device_id_type=MESH,
        )

    def t_start(a):
        @pl.loop(1, FRAMES)
        def _(i):
            t_copy(a, i).start()

    t_start(0)
    t_start(1)
    loads[0].wait()
    row = lax.broadcasted_iota(jnp.int32, (TOKENS, TOKENS), 0)
    col = lax.broadcasted_iota(jnp.int32, (TOKENS, TOKENS), 1)
    for clip in range(CLIPS):
        diagonal = jnp.where(row == col, mask[clip].astype(F32), 0.0).astype(BF16)
        masked = dot(diagonal, sin[3, clip])
        cot[8 * clip:8 * clip + 8] = masked.reshape(8, GROUPS, 8, D).astype(BF16)
    t_start(2)
    t_start(3)
    own = [
        pltpu.make_async_copy(sources[a].at[mf], tin.at[a, mf], local_sem.at[6 + a]) for a in range(4)
    ]
    for copy in own:
        copy.start()

    for a in range(3):
        loads[1 + a].wait()

    @pl.loop(0, 3)
    def _(a):
        x = sin.at[a]
        main0 = x[0, 0:128, :].astype(F32).T
        main1 = x[1, 0:128, :].astype(F32).T
        third = jnp.concatenate([x[0, 128:192, :].astype(F32), x[1, 128:192, :].astype(F32)], axis=0).T
        store_slabs(send.at[a], main0, main1, third)
        for clip in range(CLIPS):
            own_copy(a, clip).start()
            for i in (2, 4, 6):
                s_copy(a, i, clip).start()

    row = lax.broadcasted_iota(jnp.int32, (ROWS, ROWS), 0)
    col = lax.broadcasted_iota(jnp.int32, (ROWS, ROWS), 1)
    offset = jnp.full((ROWS, ROWS), FRAMES - 1, jnp.int32)
    for f in range(FRAMES):
        offset = offset + jnp.where((row >> 3) == f, order[f], 0) - jnp.where((col >> 3) == f, order[f], 0)
    offset = jnp.where((row & 7) == (col & 7), offset, -1)

    @pl.loop(0, HEADS)
    def _(h):
        total = jnp.full((ROWS, ROWS), -1e30, F32)
        for o in range(2 * FRAMES - 1):
            total = jnp.where(offset == o, rel_bias[h, o] * LOG2E, total)
        bias[h] = total

    for a in range(4):
        own[a].wait()

        @pl.loop(1, FRAMES)
        def _(i):
            t_copy(a, i).wait()

    for a in range(2):
        for clip in range(CLIPS):
            for i in (1, 7, 3, 5):
                s_copy(a, i, clip).start()

    lane = lax.broadcasted_iota(jnp.int32, (1, 256), 1)

    @pl.loop(0, GROUPS)
    def _(g):
        for a in range(4):
            xg[a] = tin[a, :, g].astype(F32).reshape(ROWS, D).astype(BF16)
        carry = None
        for p in range(SPACE):
            window = slice(128 * p, 128 * p + 256)
            first = 16 * p
            m0 = jnp.where((lane >= first) & (lane < first + E), 1.0, 0.0).astype(BF16)
            m1 = jnp.where((lane >= first + E) & (lane < first + 2 * E), 1.0, 0.0).astype(BF16)

            def stacked(x):
                return jnp.concatenate([x * m0, x * m1], axis=0)

            q, k, c, v = (xg[a, :, window] for a in range(4))
            k2 = stacked(k)
            scores = dot(q, k2, NT)
            dprob = dot(c, stacked(v), NT)
            ds, low_t, ds_t = [], [], []
            for n in range(2):
                part = slice(128 * n, 128 * n + 128)
                pr = softmax(scores[:, part] * (SCALE * LOG2E) + bias[2 * p + n])
                low = pr.astype(BF16)
                d = score_grads(pr, low, dprob[:, part])
                ds.append(d)
                low_t.append(low.astype(F32).T.astype(BF16))
                ds_t.append(d.astype(F32).T.astype(BF16))
            outs = (
                dot(jnp.concatenate(ds, axis=1), k2) * SCALE,
                dot(jnp.concatenate(ds_t, axis=1), stacked(q)) * SCALE,
                dot(jnp.concatenate(low_t, axis=1), stacked(c)),
            )
            rows = pl.ds(pl.multiple_of(g * ROWS, ROWS), ROWS)
            for n, out in enumerate(outs):
                left = out[:, :128] if carry is None else out[:, :128] + carry[n]
                joined[rows, D * n + 128 * p:D * n + 128 * p + 128] = left.astype(BF16)
                if p == SPACE - 1:
                    joined[rows, D * n + 1024:D * n + D] = out[:, 128:].astype(BF16)
            carry = [out[:, 128:] for out in outs]

    loads[4].wait()
    mid = dot(joined[...], wq[...], NT)
    for g in range(GROUPS):
        gm_send[:, g] = mid[g * ROWS:(g + 1) * ROWS].reshape(FRAMES, 8, D).astype(BF16)

    @pl.loop(1, FRAMES)
    def _(i):
        g_copy(i).start()

    own_gm = pltpu.make_async_copy(gm_send.at[mf], gm_in.at[mf], local_sem.at[10])
    own_gm.start()
    for i in (1, 7, 3, 5):
        s_copy(2, i, 0).start()
    own_gm.wait()

    @pl.loop(1, FRAMES)
    def _(i):
        g_copy(i).wait()

    gm_out = pltpu.make_async_copy(gm_in, gm, local_sem.at[11])
    gm_out.start()
    loads[5].wait()
    mid = gm_in[...].astype(F32).reshape(CLIPS, TOKENS, D)
    mid = jnp.concatenate([mid[0, :128], mid[1, :128], mid[0, 128:], mid[1, 128:]], axis=0).astype(BF16)
    cot_t = dot(wo[...], mid, NT)
    store_slabs(send.at[3], cot_t[:, :128], cot_t[:, 128:256], cot_t[:, 256:])
    for clip in range(CLIPS):
        if clip == 1:
            for i in (1, 7, 3, 5):
                s_copy(2, i, 1).start()
        own_copy(3, clip).start()
        for i in (1, 7, 3, 5, 2, 4, 6):
            s_copy(3, i, clip).start()

    def gather(a, clip, head, dst):
        for s in range(SPACE):
            dst[:, 128 * s:128 * s + 128] = recv[a, s, clip, head]
        for m in range(SPACE // 2):
            low = recv[a, 2 * m, clip, 2].astype(F32)
            high = recv[a, 2 * m + 1, clip, 2].astype(F32)
            if head == 0:
                high = pltpu.roll(high, 64, 1)
            else:
                low = pltpu.roll(low, 64, 1)
            dst[:, 1024 + 128 * m:1152 + 128 * m] = halves(low, high).astype(BF16)

    @pl.loop(0, CLIPS)
    def _(clip):
        s_wait(0, clip)
        s_wait(1, clip)
        for head in range(2):
            gather(0, clip, head, q_t)
            gather(1, clip, head, k_t)
            row_n[...] = q_t[...].astype(F32).T.astype(BF16)
            for b in range(SEQ // BLOCK):
                block = slice(b * BLOCK, (b + 1) * BLOCK)
                scores = dot(row_n[block], k_t[...]) * (SCALE * LOG2E)
                probs[2 * clip + head, block] = softmax(scores).astype(BF16)

    def scatter(a, clip, head, tile, value):
        if tile < SPACE:
            send[a, tile, clip, head] = value.astype(BF16)
        elif head == 0:
            thirds[a, tile - SPACE] = value
        else:
            m = tile - SPACE
            other = thirds[a, m]
            send[a, 2 * m, clip, 2] = halves(other, pltpu.roll(value, 64, 1)).astype(BF16)
            send[a, 2 * m + 1, clip, 2] = halves(pltpu.roll(other, 64, 1), value).astype(BF16)

    @pl.loop(0, CLIPS)
    def _(clip):
        s_wait(2, clip)
        s_wait(3, clip)
        for head in range(2):
            for a, dst in enumerate((q_t, k_t, v_t, c_t)):
                gather(a, clip, head, dst)
            row_n[...] = c_t[...].astype(F32).T.astype(BF16)
            for b in range(SEQ // BLOCK):
                block = slice(b * BLOCK, (b + 1) * BLOCK)
                low = probs[2 * clip + head, block]
                ds = score_grads(low.astype(F32), low, dot(row_n[block], v_t[...]))
                to_q = dot(k_t[...], ds, NT) * SCALE
                for n in range(BLOCK // 128):
                    scatter(0, clip, head, b * (BLOCK // 128) + n, to_q[:, 128 * n:128 * n + 128])
                to_k = dot(q_t[:, block], ds)
                to_v = dot(c_t[:, block], low)
                if b > 0:
                    to_k, to_v = sum_k[...] + to_k, sum_v[...] + to_v
                if b < SEQ // BLOCK - 1:
                    sum_k[...], sum_v[...] = to_k, to_v
            to_k = to_k * SCALE
            for n in range(SEQ // 128):
                scatter(1, clip, head, n, to_k[:, 128 * n:128 * n + 128])
                scatter(2, clip, head, n, to_v[:, 128 * n:128 * n + 128])
            for slab in (0,) if head == 0 else (1, 2):
                for a in range(3):
                    for i in (1, 7, 3, 5, 2, 4, 6):
                        b_copy(a, i, clip, slab).start()

    outs = []
    for clip in range(CLIPS):
        own = [
            pltpu.make_async_copy(send.at[a, ms, clip], back.at[a, ms, clip], local_sem.at[a])
            for a in range(3)
        ]
        for copy in own:
            copy.start()
        for a, out in enumerate((gq, gk, gv)):
            own[a].wait()

            @pl.loop(1, SPACE)
            def _(i):
                for slab in range(3):
                    b_copy(a, i, clip, slab).wait()

            main = back[a, :, clip, 0:2].astype(F32).reshape(D, 128)
            sin[a, clip, 0:128, :] = main.T.astype(BF16)
            third = back[a, :, clip, 2].astype(F32)
            odd = pltpu.roll(third.reshape(SPACE * E, 128), 64, 1).reshape(SPACE, 1, E, 128)
            third = jnp.concatenate([third.reshape(SPACE, 1, E, 128), odd], axis=1).reshape(D, 128)
            sin[a, clip, 128:192, :] = third.T[0:64].astype(BF16)
            outs.append(pltpu.make_async_copy(sin.at[a, clip], out.at[clip], out_sem.at[a, clip]))
            outs[-1].start()
    gm_out.wait()
    for copy in outs:
        copy.wait()


def copy_kernel(a, b, c, d, a_out, b_out, c_out, d_out, held, in_sem, out_sem):
    pairs = ((a, a_out), (b, b_out), (c, c_out), (d, d_out))
    reads = [pltpu.make_async_copy(src, held.at[n], in_sem.at[n]) for n, (src, _) in enumerate(pairs)]
    writes = [pltpu.make_async_copy(held.at[n], dst, out_sem.at[n]) for n, (_, dst) in enumerate(pairs)]
    for copy in reads:
        copy.start()
    for read, write in zip(reads, writes):
        read.wait()
        write.start()
    for copy in writes:
        copy.wait()


def on_device(
    q_spatial, k_spatial, v_spatial, q_temporal, k_temporal, v_temporal, grad_out,
    inpaint_mask, frame_order, rel_bias, w_qkv, w_out,
):
    chunks = (FRAMES, GROUPS, 8, D)
    shape = (CLIPS, TOKENS, D)
    slabs = (SPACE, CLIPS, 3, E, 128)
    hbm = pl.BlockSpec(memory_space=pl.ANY)
    vmem = pl.BlockSpec(memory_space=pltpu.VMEM)
    smem = pl.BlockSpec(memory_space=pltpu.SMEM)
    dma = pltpu.SemaphoreType.DMA
    results = pl.pallas_call(
        kernel,
        out_shape=(jax.ShapeDtypeStruct(shape, BF16),) * 3 + (jax.ShapeDtypeStruct(chunks, BF16),),
        in_specs=[hbm, hbm, hbm, hbm, vmem, smem, smem, hbm, hbm, hbm, hbm, hbm],
        out_specs=(hbm,) * 4,
        scratch_shapes=[
            pltpu.VMEM(chunks, BF16),
            pltpu.VMEM((4,) + chunks, BF16),
            pltpu.VMEM((4, ROWS, D), BF16),
            pltpu.VMEM((HEADS, ROWS, ROWS), F32),
            pltpu.VMEM((GROUPS * ROWS, 3 * D), BF16),
            pltpu.VMEM(chunks, BF16),
            pltpu.VMEM(chunks, BF16),
            pltpu.VMEM((4,) + shape, BF16),
            pltpu.VMEM((4,) + slabs, BF16),
            pltpu.VMEM((4,) + slabs, BF16),
            pltpu.VMEM((3,) + slabs, BF16),
            pltpu.VMEM((D, 3 * D), BF16),
            pltpu.VMEM((D, D), BF16),
            pltpu.VMEM((4, SEQ, SEQ), BF16),
            *(pltpu.VMEM((E, SEQ), BF16) for _ in range(4)),
            pltpu.VMEM((SEQ, E), BF16),
            *(pltpu.VMEM((E, SEQ), F32) for _ in range(2)),
            pltpu.VMEM((3, 4, E, 128), F32),
            dma((4, FRAMES)), dma((4, FRAMES)), dma((FRAMES,)), dma((FRAMES,)),
            dma((4, SPACE, CLIPS)), dma((4, SPACE, CLIPS)),
            dma((3, SPACE, CLIPS, 3)), dma((3, SPACE, CLIPS, 3)),
            dma((12,)), dma((4, CLIPS)), dma((3, CLIPS)),
        ],
        compiler_params=pltpu.CompilerParams(
            collective_id=0, has_side_effects=True, vmem_limit_bytes=63 * 2**20
        ),
    )(
        q_temporal.reshape(chunks), k_temporal.reshape(chunks), v_temporal.reshape(chunks),
        grad_out.reshape(shape), inpaint_mask, frame_order, rel_bias,
        q_spatial.reshape(shape), k_spatial.reshape(shape), v_spatial.reshape(shape), w_qkv, w_out,
    )
    flat = (CLIPS * TOKENS, D)
    results = pl.pallas_call(
        copy_kernel,
        out_shape=(jax.ShapeDtypeStruct(flat, BF16),) * 4,
        in_specs=[hbm] * 4,
        out_specs=(hbm,) * 4,
        scratch_shapes=[pltpu.VMEM((4,) + flat, BF16), dma((4,)), dma((4,))],
    )(*(r.reshape(flat) for r in results))
    return tuple(r.reshape(CLIPS, 1, TOKENS, D) for r in results)


def solution(mesh):
    split = P(None, "frame", "space", None)
    in_specs = (split,) * 7 + (P(None, "frame", "space"), P(), P(), P(), P())
    return jax.shard_map(
        on_device, mesh=mesh, in_specs=in_specs, out_specs=(split,) * 4, check_vma=False
    )
```

```python
import jax
import jax.numpy as jnp
from jax import lax
from jax.experimental import pallas as pl
from jax.experimental.pallas import tpu as pltpu
from jax.sharding import PartitionSpec as P

HEADS = 16
E = 72
D = 1152
CLIPS = 2
FRAMES = 16
TOKENS = 192
SEQ = 1536
SPACE = 8
GROUPS = 3
ROWS = 128
BLOCK = 512
SCALE = E ** (-0.5)
LOG2E = 1.4426950408889634
MESH = pl.DeviceIdType.MESH
NN = (((1,), (0,)), ((), ()))
NT = (((1,), (1,)), ((), ()))
F32 = jnp.float32
BF16 = jnp.bfloat16


def dot(a, b, dims=NN):
    return lax.dot_general(a, b, dims, preferred_element_type=F32)


def softmax(scores):
    weights = jnp.exp2(scores - jnp.max(scores, axis=1, keepdims=True))
    return weights * (1.0 / jnp.sum(weights, axis=1, keepdims=True))


def score_grads(probs, probs_low, dprob):
    delta = jnp.sum(probs_low.astype(F32) * dprob, axis=1, keepdims=True)
    return (probs * (dprob - delta)).astype(BF16)


def halves(low, high):
    lane = lax.broadcasted_iota(jnp.int32, low.shape, 1)
    return jnp.where(lane < 64, low, high)


def store_slabs(dst, main0, main1, third):
    for clip, main in enumerate((main0, main1)):
        by_head = main.reshape(SPACE, 2, E, 128)
        dst[:, clip, 0] = by_head[:, 0].astype(BF16)
        dst[:, clip, 1] = by_head[:, 1].astype(BF16)
    by_head = third.reshape(SPACE, 2, E, 128)
    even = by_head[:, 0].reshape(SPACE * E, 128)
    odd = by_head[:, 1].reshape(SPACE * E, 128)
    dst[:, 0, 2] = halves(even, pltpu.roll(odd, 64, 1)).reshape(SPACE, E, 128).astype(BF16)
    dst[:, 1, 2] = halves(pltpu.roll(even, 64, 1), odd).reshape(SPACE, E, 128).astype(BF16)


def kernel(
    qt, kt, vt, go, mask, order, rel_bias, qs, ks, vs, wqkv, wout,
    gq, gk, gv, gm,
    cot, tin, bias, joined, gm_in, sin, send, recv, back, wq, wo,
    probs, q_t, k_t, v_t, c_t, row_n, sum_k, sum_v, thirds,
    t_send_sem, t_recv_sem, g_send_sem, g_recv_sem, s_send_sem, s_recv_sem, b_send_sem, b_recv_sem,
    local_sem, own_sem, out_sem,
):
    mf, ms = lax.axis_index("frame"), lax.axis_index("space")
    barrier = pltpu.get_barrier_semaphore()

    @pl.loop(1, FRAMES)
    def _(i):
        pl.semaphore_signal(barrier, inc=1, device_id=(lax.rem(mf + i, FRAMES), ms), device_id_type=MESH)

    @pl.loop(1, SPACE)
    def _(i):
        pl.semaphore_signal(barrier, inc=1, device_id=(mf, lax.rem(ms + i, SPACE)), device_id_type=MESH)

    loads = [
        pltpu.make_async_copy(src, dst, local_sem.at[n])
        for n, (src, dst) in enumerate(
            ((go, cot), (qs, sin.at[0]), (ks, sin.at[1]), (vs, sin.at[2]), (wqkv, wq), (wout, wo))
        )
    ]
    loads[0].start()
    pl.semaphore_wait(barrier, FRAMES + SPACE - 2)

    sources = (qt, kt, cot, vt)

    def t_start(a, g):
        @pl.loop(1, FRAMES)
        def _(i):
            peer = lax.rem(mf + i, FRAMES)
            pltpu.make_async_remote_copy(
                src_ref=sources[a].at[peer, g], dst_ref=tin.at[a, mf, g],
                send_sem=t_send_sem.at[a, g], recv_sem=t_recv_sem.at[a, g],
                device_id=(peer, ms), device_id_type=MESH,
            ).start()
        pltpu.make_async_copy(sources[a].at[mf, g], tin.at[a, mf, g], own_sem.at[a, g]).start()

    def t_wait(a, g):
        some = tin.at[a, 0:FRAMES - 1, g]
        sems = (t_send_sem.at[a, g], t_recv_sem.at[a, g])
        pltpu.make_async_copy(sources[a].at[mf, g], tin.at[a, mf, g], own_sem.at[a, g]).wait()
        for sem in sems:
            pltpu.make_async_copy(some, some, sem).wait()

    def g_start(g):
        @pl.loop(1, FRAMES)
        def _(i):
            peer = lax.rem(mf + i, FRAMES)
            pltpu.make_async_remote_copy(
                src_ref=tin.at[0, peer, g], dst_ref=gm_in.at[mf, g],
                send_sem=g_send_sem.at[g], recv_sem=g_recv_sem.at[g],
                device_id=(peer, ms), device_id_type=MESH,
            ).start()
        pltpu.make_async_copy(tin.at[0, mf, g], gm_in.at[mf, g], own_sem.at[4, g]).start()

    def g_wait(g):
        some = gm_in.at[0:FRAMES - 1, g]
        sems = (g_send_sem.at[g], g_recv_sem.at[g])
        pltpu.make_async_copy(tin.at[0, mf, g], gm_in.at[mf, g], own_sem.at[4, g]).wait()
        for sem in sems:
            pltpu.make_async_copy(some, some, sem).wait()

    def s_start(a, clip):
        pltpu.make_async_copy(send.at[a, ms, clip], recv.at[a, ms, clip], own_sem.at[5 + a, clip]).start()
        for i in (1, 7, 3, 5, 2, 4, 6):
            peer = lax.rem(ms + i, SPACE)
            pltpu.make_async_remote_copy(
                src_ref=send.at[a, peer, clip], dst_ref=recv.at[a, ms, clip],
                send_sem=s_send_sem.at[a, clip], recv_sem=s_recv_sem.at[a, clip],
                device_id=(mf, peer), device_id_type=MESH,
            ).start()

    def s_wait(a, clip):
        some = recv.at[a, 0:SPACE - 1, clip]
        sems = (s_send_sem.at[a, clip], s_recv_sem.at[a, clip])
        pltpu.make_async_copy(send.at[a, ms, clip], recv.at[a, ms, clip], own_sem.at[5 + a, clip]).wait()
        for sem in sems:
            pltpu.make_async_copy(some, some, sem).wait()

    def b_start(a, peer, clip, slab):
        @pl.when(peer != ms)
        def _():
            pltpu.make_async_remote_copy(
                src_ref=send.at[a, peer, clip, slab], dst_ref=back.at[a, ms, clip, slab],
                send_sem=b_send_sem.at[a, clip], recv_sem=b_recv_sem.at[a, clip],
                device_id=(mf, peer), device_id_type=MESH,
            ).start()

    def b_start_all(a, clip, slab):
        for i in (1, 7, 3, 5, 2, 4, 6):
            peer = lax.rem(ms + i, SPACE)
            pltpu.make_async_remote_copy(
                src_ref=send.at[a, peer, clip, slab], dst_ref=back.at[a, ms, clip, slab],
                send_sem=b_send_sem.at[a, clip], recv_sem=b_recv_sem.at[a, clip],
                device_id=(mf, peer), device_id_type=MESH,
            ).start()

    def b_wait(a, clip):
        some = back.at[a, 0:SPACE - 1, clip]
        sems = (b_send_sem.at[a, clip], b_recv_sem.at[a, clip])
        for sem in sems:
            pltpu.make_async_copy(some, some, sem).wait()

    t_start(0, 0)
    t_start(1, 0)
    t_start(3, 0)
    loads[0].wait()
    row = lax.broadcasted_iota(jnp.int32, (TOKENS, TOKENS), 0)
    col = lax.broadcasted_iota(jnp.int32, (TOKENS, TOKENS), 1)
    for clip in range(CLIPS):
        diagonal = jnp.where(row == col, mask[clip].astype(F32), 0.0).astype(BF16)
        masked = dot(diagonal, cot[8 * clip:8 * clip + 8].astype(F32).reshape(TOKENS, D).astype(BF16))
        cot[8 * clip:8 * clip + 8] = masked.reshape(8, GROUPS, 8, D).astype(BF16)
    t_start(2, 0)
    for g in range(1, GROUPS):
        for a in range(4):
            t_start(a, g)
    for copy in loads[1:]:
        copy.start()

    row = lax.broadcasted_iota(jnp.int32, (ROWS, ROWS), 0)
    col = lax.broadcasted_iota(jnp.int32, (ROWS, ROWS), 1)
    offset = jnp.full((ROWS, ROWS), FRAMES - 1, jnp.int32)
    for f in range(FRAMES):
        offset = offset + jnp.where((row >> 3) == f, order[f], 0) - jnp.where((col >> 3) == f, order[f], 0)
    offset = jnp.where((row & 7) == (col & 7), offset, -1)

    @pl.loop(0, HEADS)
    def _(h):
        total = jnp.full((ROWS, ROWS), -1e30, F32)
        for o in range(2 * FRAMES - 1):
            total = jnp.where(offset == o, rel_bias[h, o] * LOG2E, total)
        bias[h] = total

    for copy in loads[1:]:
        copy.wait()

    @pl.loop(0, 3)
    def _(a):
        x = sin.at[a]
        main0 = x[0, 0:128, :].astype(F32).T
        main1 = x[1, 0:128, :].astype(F32).T
        third = jnp.concatenate([x[0, 128:192, :].astype(F32), x[1, 128:192, :].astype(F32)], axis=0).T
        store_slabs(send.at[a], main0, main1, third)

    lane = lax.broadcasted_iota(jnp.int32, (1, 256), 1)

    @pl.loop(0, GROUPS)
    def _(g):
        for a in range(4):
            t_wait(a, g)

        @pl.when(g == GROUPS - 1)
        def _():
            s_start(0, 0)
            s_start(1, 0)

        carry = None
        for p in range(SPACE):
            window = slice(128 * p, 128 * p + 256)
            first = 16 * p
            m0 = jnp.where((lane >= first) & (lane < first + E), 1.0, 0.0).astype(BF16)
            m1 = jnp.where((lane >= first + E) & (lane < first + 2 * E), 1.0, 0.0).astype(BF16)

            def stacked(x):
                return jnp.concatenate([x * m0, x * m1], axis=0)

            q, k, c, v = (
                tin[a, :, g, :, window].astype(F32).reshape(ROWS, 256).astype(BF16) for a in range(4)
            )
            k2 = stacked(k)
            scores = dot(q, k2, NT)
            dprob = dot(c, stacked(v), NT)
            ds, low_t, ds_t = [], [], []
            for n in range(2):
                part = slice(128 * n, 128 * n + 128)
                pr = softmax(scores[:, part] * (SCALE * LOG2E) + bias[2 * p + n])
                low = pr.astype(BF16)
                d = score_grads(pr, low, dprob[:, part])
                ds.append(d)
                low_t.append(low.astype(F32).T.astype(BF16))
                ds_t.append(d.astype(F32).T.astype(BF16))
            outs = (
                dot(jnp.concatenate(ds, axis=1), k2) * SCALE,
                dot(jnp.concatenate(ds_t, axis=1), stacked(q)) * SCALE,
                dot(jnp.concatenate(low_t, axis=1), stacked(c)),
            )
            for n, out in enumerate(outs):
                left = out[:, :128] if carry is None else out[:, :128] + carry[n]
                joined[:, D * n + 128 * p:D * n + 128 * p + 128] = left.astype(BF16)
                if p == SPACE - 1:
                    joined[:, D * n + 1024:D * n + D] = out[:, 128:].astype(BF16)
            carry = [out[:, 128:] for out in outs]
        tin[0, :, g] = dot(joined[...], wq[...], NT).reshape(FRAMES, 8, D).astype(BF16)
        g_start(g)

    s_start(2, 0)
    for g in range(GROUPS):
        g_wait(g)
    gm_out = pltpu.make_async_copy(gm_in, gm, local_sem.at[6])
    gm_out.start()
    mid = gm_in[...].astype(F32).reshape(CLIPS, TOKENS, D)
    mid = jnp.concatenate([mid[0, :128], mid[1, :128], mid[0, 128:], mid[1, 128:]], axis=0).astype(BF16)
    cot_t = dot(wo[...], mid, NT)
    store_slabs(send.at[3], cot_t[:, :128], cot_t[:, 128:256], cot_t[:, 256:])
    s_start(3, 0)
    for a in range(4):
        s_start(a, 1)

    def gather(a, clip, head, dst):
        for s in range(SPACE):
            dst[:, 128 * s:128 * s + 128] = recv[a, s, clip, head]
        for m in range(SPACE // 2):
            low = recv[a, 2 * m, clip, 2].astype(F32)
            high = recv[a, 2 * m + 1, clip, 2].astype(F32)
            if head == 0:
                high = pltpu.roll(high, 64, 1)
            else:
                low = pltpu.roll(low, 64, 1)
            dst[:, 1024 + 128 * m:1152 + 128 * m] = halves(low, high).astype(BF16)

    def scatter(a, clip, head, tile, value):
        if tile < SPACE:
            send[a, tile, clip, head] = value.astype(BF16)
        elif head == 0:
            thirds[a, tile - SPACE] = value
        else:
            m = tile - SPACE
            other = thirds[a, m]
            send[a, 2 * m, clip, 2] = halves(other, pltpu.roll(value, 64, 1)).astype(BF16)
            send[a, 2 * m + 1, clip, 2] = halves(pltpu.roll(other, 64, 1), value).astype(BF16)

    @pl.loop(0, CLIPS)
    def _(clip):
        s_wait(0, clip)
        s_wait(1, clip)
        for head in range(2):
            gather(0, clip, head, q_t.at[head])
            gather(1, clip, head, k_t.at[head])
            row_n[...] = q_t[head].astype(F32).T.astype(BF16)
            for b in range(SEQ // BLOCK):
                block = slice(b * BLOCK, (b + 1) * BLOCK)
                scores = dot(row_n[block], k_t[head]) * (SCALE * LOG2E)
                probs[head, block] = softmax(scores).astype(BF16)
        s_wait(2, clip)
        s_wait(3, clip)
        for head in range(2):
            gather(2, clip, head, v_t)
            gather(3, clip, head, c_t)
            row_n[...] = c_t[...].astype(F32).T.astype(BF16)
            for b in range(SEQ // BLOCK):
                block = slice(b * BLOCK, (b + 1) * BLOCK)
                low = probs[head, block]
                ds = score_grads(low.astype(F32), low, dot(row_n[block], v_t[...]))
                to_q = dot(k_t[head], ds, NT) * SCALE
                for n in range(BLOCK // 128):
                    tile = b * (BLOCK // 128) + n
                    scatter(0, clip, head, tile, to_q[:, 128 * n:128 * n + 128])
                    if tile < SPACE:
                        b_start(0, tile, clip, head)
                to_k = dot(q_t[head, :, block], ds)
                to_v = dot(c_t[:, block], low)
                if b > 0:
                    to_k, to_v = sum_k[...] + to_k, sum_v[...] + to_v
                if b < SEQ // BLOCK - 1:
                    sum_k[...], sum_v[...] = to_k, to_v
            to_k = to_k * SCALE
            for n in range(SEQ // 128):
                scatter(1, clip, head, n, to_k[:, 128 * n:128 * n + 128])
                scatter(2, clip, head, n, to_v[:, 128 * n:128 * n + 128])
            b_start_all(1, clip, head)
            b_start_all(2, clip, head)
            if head == 1:
                for a in range(3):
                    b_start_all(a, clip, 2)

    outs = []
    for clip in range(CLIPS):
        own = [
            pltpu.make_async_copy(send.at[a, ms, clip], back.at[a, ms, clip], local_sem.at[a])
            for a in range(3)
        ]
        for copy in own:
            copy.start()
        for a, out in enumerate((gq, gk, gv)):
            own[a].wait()
            b_wait(a, clip)
            main = back[a, :, clip, 0:2].astype(F32).reshape(D, 128)
            sin[a, clip, 0:128, :] = main.T.astype(BF16)
            third = back[a, :, clip, 2].astype(F32)
            odd = pltpu.roll(third.reshape(SPACE * E, 128), 64, 1).reshape(SPACE, 1, E, 128)
            third = jnp.concatenate([third.reshape(SPACE, 1, E, 128), odd], axis=1).reshape(D, 128)
            sin[a, clip, 128:192, :] = third.T[0:64].astype(BF16)
            outs.append(pltpu.make_async_copy(sin.at[a, clip], out.at[clip], out_sem.at[a, clip]))
            outs[-1].start()
    gm_out.wait()
    for copy in outs:
        copy.wait()


def copy_kernel(a, b, c, d, a_out, b_out, c_out, d_out, held, in_sem, out_sem):
    pairs = ((a, a_out), (b, b_out), (c, c_out), (d, d_out))
    reads = [pltpu.make_async_copy(src, held.at[n], in_sem.at[n]) for n, (src, _) in enumerate(pairs)]
    writes = [pltpu.make_async_copy(held.at[n], dst, out_sem.at[n]) for n, (_, dst) in enumerate(pairs)]
    for copy in reads:
        copy.start()
    for read, write in zip(reads, writes):
        read.wait()
        write.start()
    for copy in writes:
        copy.wait()


def on_device(
    q_spatial, k_spatial, v_spatial, q_temporal, k_temporal, v_temporal, grad_out,
    inpaint_mask, frame_order, rel_bias, w_qkv, w_out,
):
    chunks = (FRAMES, GROUPS, 8, D)
    shape = (CLIPS, TOKENS, D)
    slabs = (SPACE, CLIPS, 3, E, 128)
    hbm = pl.BlockSpec(memory_space=pl.ANY)
    vmem = pl.BlockSpec(memory_space=pltpu.VMEM)
    smem = pl.BlockSpec(memory_space=pltpu.SMEM)
    dma = pltpu.SemaphoreType.DMA
    results = pl.pallas_call(
        kernel,
        out_shape=(jax.ShapeDtypeStruct(shape, BF16),) * 3 + (jax.ShapeDtypeStruct(chunks, BF16),),
        in_specs=[hbm, hbm, hbm, hbm, vmem, smem, smem, hbm, hbm, hbm, hbm, hbm],
        out_specs=(hbm,) * 4,
        scratch_shapes=[
            pltpu.VMEM(chunks, BF16),
            pltpu.VMEM((4,) + chunks, BF16),
            pltpu.VMEM((HEADS, ROWS, ROWS), F32),
            pltpu.VMEM((ROWS, 3 * D), BF16),
            pltpu.VMEM(chunks, BF16),
            pltpu.VMEM((3,) + shape, BF16),
            pltpu.VMEM((4,) + slabs, BF16),
            pltpu.VMEM((4,) + slabs, BF16),
            pltpu.VMEM((3,) + slabs, BF16),
            pltpu.VMEM((D, 3 * D), BF16),
            pltpu.VMEM((D, D), BF16),
            pltpu.VMEM((2, SEQ, SEQ), BF16),
            *(pltpu.VMEM((2, E, SEQ), BF16) for _ in range(2)),
            *(pltpu.VMEM((E, SEQ), BF16) for _ in range(2)),
            pltpu.VMEM((SEQ, E), BF16),
            *(pltpu.VMEM((E, SEQ), F32) for _ in range(2)),
            pltpu.VMEM((3, 4, E, 128), F32),
            dma((4, GROUPS)), dma((4, GROUPS)), dma((GROUPS,)), dma((GROUPS,)),
            dma((4, CLIPS)), dma((4, CLIPS)), dma((3, CLIPS)), dma((3, CLIPS)),
            dma((7,)), dma((9, GROUPS)), dma((3, CLIPS)),
        ],
        compiler_params=pltpu.CompilerParams(
            collective_id=0, has_side_effects=True, vmem_limit_bytes=63 * 2**20
        ),
    )(
        q_temporal.reshape(chunks), k_temporal.reshape(chunks), v_temporal.reshape(chunks),
        grad_out.reshape(chunks), inpaint_mask, frame_order, rel_bias,
        q_spatial.reshape(shape), k_spatial.reshape(shape), v_spatial.reshape(shape), w_qkv, w_out,
    )
    flat = (CLIPS * TOKENS, D)
    results = pl.pallas_call(
        copy_kernel,
        out_shape=(jax.ShapeDtypeStruct(flat, BF16),) * 4,
        in_specs=[hbm] * 4,
        out_specs=(hbm,) * 4,
        scratch_shapes=[pltpu.VMEM((4,) + flat, BF16), dma((4,)), dma((4,))],
    )(*(r.reshape(flat) for r in results))
    return tuple(r.reshape(CLIPS, 1, TOKENS, D) for r in results)


def solution(mesh):
    split = P(None, "frame", "space", None)
    in_specs = (split,) * 7 + (P(None, "frame", "space"), P(), P(), P(), P())
    return jax.shard_map(
        on_device, mesh=mesh, in_specs=in_specs, out_specs=(split,) * 4, check_vma=False
    )
```

```python
import jax
import jax.numpy as jnp
from jax import lax
from jax.experimental import pallas as pl
from jax.experimental.pallas import tpu as pltpu
from jax.sharding import PartitionSpec as P

HEADS = 16
E = 72
D = 1152
CLIPS = 2
FRAMES = 16
TOKENS = 192
SEQ = 1536
SPACE = 8
GROUPS = 3
ROWS = 128
BLOCK = 512
SCALE = E ** (-0.5)
LOG2E = 1.4426950408889634
MESH = pl.DeviceIdType.MESH
NN = (((1,), (0,)), ((), ()))
NT = (((1,), (1,)), ((), ()))
F32 = jnp.float32
BF16 = jnp.bfloat16


def dot(a, b, dims=NN):
    return lax.dot_general(a, b, dims, preferred_element_type=F32)


def softmax(scores):
    weights = jnp.exp2(scores - jnp.max(scores, axis=1, keepdims=True))
    return weights * (1.0 / jnp.sum(weights, axis=1, keepdims=True))


def score_grads(probs, probs_low, dprob):
    delta = jnp.sum(probs_low.astype(F32) * dprob, axis=1, keepdims=True)
    return (probs * (dprob - delta)).astype(BF16)


def halves(low, high):
    lane = lax.broadcasted_iota(jnp.int32, low.shape, 1)
    return jnp.where(lane < 64, low, high)


def store_slabs(dst, main0, main1, third):
    for clip, main in enumerate((main0, main1)):
        by_head = main.reshape(SPACE, 2, E, 128)
        dst[:, clip, 0] = by_head[:, 0].astype(BF16)
        dst[:, clip, 1] = by_head[:, 1].astype(BF16)
    by_head = third.reshape(SPACE, 2, E, 128)
    even = by_head[:, 0].reshape(SPACE * E, 128)
    odd = by_head[:, 1].reshape(SPACE * E, 128)
    dst[:, 0, 2] = halves(even, pltpu.roll(odd, 64, 1)).reshape(SPACE, E, 128).astype(BF16)
    dst[:, 1, 2] = halves(pltpu.roll(even, 64, 1), odd).reshape(SPACE, E, 128).astype(BF16)


def kernel(
    qt, kt, vt, go, mask_in, order_in, bias_in, qs, ks, vs, wqkv, wout,
    gq, gk, gv, gm,
    mask, order, rel_bias, cot, tin, bias, joined, gm_in, sin, send, recv, back, wq, wo,
    probs, q_t, k_t, v_t, c_t, row_n, sum_k, sum_v, thirds,
    t_send_sem, t_recv_sem, g_send_sem, g_recv_sem, s_send_sem, s_recv_sem, b_send_sem, b_recv_sem,
    local_sem, own_sem, out_sem,
):
    mf, ms = lax.axis_index("frame"), lax.axis_index("space")
    barrier = pltpu.get_barrier_semaphore()

    @pl.loop(1, FRAMES)
    def _(i):
        pl.semaphore_signal(barrier, inc=1, device_id=(lax.rem(mf + i, FRAMES), ms), device_id_type=MESH)

    @pl.loop(1, SPACE)
    def _(i):
        pl.semaphore_signal(barrier, inc=1, device_id=(mf, lax.rem(ms + i, SPACE)), device_id_type=MESH)

    loads = [
        pltpu.make_async_copy(src, dst, local_sem.at[n])
        for n, (src, dst) in enumerate(
            (
                (go, cot), (mask_in, mask), (order_in, order), (bias_in, rel_bias),
                (qs, sin.at[0]), (ks, sin.at[1]), (vs, sin.at[2]), (wqkv, wq), (wout, wo),
            )
        )
    ]
    for copy in loads[:4]:
        copy.start()
    pl.semaphore_wait(barrier, FRAMES + SPACE - 2)

    sources = (qt, kt, cot, vt)

    def t_start(a, g):
        @pl.loop(1, FRAMES)
        def _(i):
            peer = lax.rem(mf + i, FRAMES)
            pltpu.make_async_remote_copy(
                src_ref=sources[a].at[peer, g], dst_ref=tin.at[a, mf, g],
                send_sem=t_send_sem.at[a, g], recv_sem=t_recv_sem.at[a, g],
                device_id=(peer, ms), device_id_type=MESH,
            ).start()
        pltpu.make_async_copy(sources[a].at[mf, g], tin.at[a, mf, g], own_sem.at[a, g]).start()

    def t_wait(a, g):
        some = tin.at[a, 0:FRAMES - 1, g]
        sems = (t_send_sem.at[a, g], t_recv_sem.at[a, g])
        pltpu.make_async_copy(sources[a].at[mf, g], tin.at[a, mf, g], own_sem.at[a, g]).wait()
        for sem in sems:
            pltpu.make_async_copy(some, some, sem).wait()

    def g_start(g):
        @pl.loop(1, FRAMES)
        def _(i):
            peer = lax.rem(mf + i, FRAMES)
            pltpu.make_async_remote_copy(
                src_ref=tin.at[0, peer, g], dst_ref=gm_in.at[mf, g],
                send_sem=g_send_sem.at[g], recv_sem=g_recv_sem.at[g],
                device_id=(peer, ms), device_id_type=MESH,
            ).start()
        pltpu.make_async_copy(tin.at[0, mf, g], gm_in.at[mf, g], own_sem.at[4, g]).start()

    def g_wait(g):
        some = gm_in.at[0:FRAMES - 1, g]
        sems = (g_send_sem.at[g], g_recv_sem.at[g])
        pltpu.make_async_copy(tin.at[0, mf, g], gm_in.at[mf, g], own_sem.at[4, g]).wait()
        for sem in sems:
            pltpu.make_async_copy(some, some, sem).wait()

    def s_start(a, clip):
        pltpu.make_async_copy(send.at[a, ms, clip], recv.at[a, ms, clip], own_sem.at[5 + a, clip]).start()
        for i in (1, 7, 3, 5, 2, 4, 6):
            peer = lax.rem(ms + i, SPACE)
            pltpu.make_async_remote_copy(
                src_ref=send.at[a, peer, clip], dst_ref=recv.at[a, ms, clip],
                send_sem=s_send_sem.at[a, clip], recv_sem=s_recv_sem.at[a, clip],
                device_id=(mf, peer), device_id_type=MESH,
            ).start()

    def s_wait(a, clip):
        some = recv.at[a, 0:SPACE - 1, clip]
        sems = (s_send_sem.at[a, clip], s_recv_sem.at[a, clip])
        pltpu.make_async_copy(send.at[a, ms, clip], recv.at[a, ms, clip], own_sem.at[5 + a, clip]).wait()
        for sem in sems:
            pltpu.make_async_copy(some, some, sem).wait()

    def b_start(a, peer, clip, slab):
        kind = slab // 2

        @pl.when(peer != ms)
        def _():
            pltpu.make_async_remote_copy(
                src_ref=send.at[a, peer, clip, slab], dst_ref=back.at[a, ms, clip, slab],
                send_sem=b_send_sem.at[a, clip, kind], recv_sem=b_recv_sem.at[a, clip, kind],
                device_id=(mf, peer), device_id_type=MESH,
            ).start()

    def b_start_all(a, clip, slab):
        kind = slab // 2
        for i in (1, 7, 3, 5, 2, 4, 6):
            peer = lax.rem(ms + i, SPACE)
            pltpu.make_async_remote_copy(
                src_ref=send.at[a, peer, clip, slab], dst_ref=back.at[a, ms, clip, slab],
                send_sem=b_send_sem.at[a, clip, kind], recv_sem=b_recv_sem.at[a, clip, kind],
                device_id=(mf, peer), device_id_type=MESH,
            ).start()

    def b_wait(a, clip, kind):
        some = back.at[a, 0:SPACE - 1, clip, 2 * kind:2 + kind]
        sems = (b_send_sem.at[a, clip, kind], b_recv_sem.at[a, clip, kind])
        for sem in sems:
            pltpu.make_async_copy(some, some, sem).wait()

    t_start(0, 0)
    t_start(1, 0)
    t_start(3, 0)
    for copy in loads[:4]:
        copy.wait()
    row = lax.broadcasted_iota(jnp.int32, (TOKENS, TOKENS), 0)
    col = lax.broadcasted_iota(jnp.int32, (TOKENS, TOKENS), 1)
    for clip in range(CLIPS):
        diagonal = jnp.where(row == col, mask[clip].astype(F32), 0.0).astype(BF16)
        masked = dot(diagonal, cot[8 * clip:8 * clip + 8].astype(F32).reshape(TOKENS, D).astype(BF16))
        cot[8 * clip:8 * clip + 8] = masked.reshape(8, GROUPS, 8, D).astype(BF16)
    t_start(2, 0)
    for g in range(1, GROUPS):
        for a in range(4):
            t_start(a, g)
    for copy in loads[4:]:
        copy.start()

    row = lax.broadcasted_iota(jnp.int32, (ROWS, ROWS), 0)
    col = lax.broadcasted_iota(jnp.int32, (ROWS, ROWS), 1)
    offset = jnp.full((ROWS, ROWS), FRAMES - 1, jnp.int32)
    for f in range(FRAMES):
        offset = offset + jnp.where((row >> 3) == f, order[f], 0) - jnp.where((col >> 3) == f, order[f], 0)
    offset = jnp.where((row & 7) == (col & 7), offset, -1)

    @pl.loop(0, HEADS)
    def _(h):
        total = jnp.full((ROWS, ROWS), -1e30, F32)
        for o in range(2 * FRAMES - 1):
            total = jnp.where(offset == o, rel_bias[h, o] * LOG2E, total)
        bias[h] = total

    for copy in loads[4:]:
        copy.wait()

    @pl.loop(0, 3)
    def _(a):
        x = sin.at[a]
        main0 = x[0, 0:128, :].astype(F32).T
        main1 = x[1, 0:128, :].astype(F32).T
        third = jnp.concatenate([x[0, 128:192, :].astype(F32), x[1, 128:192, :].astype(F32)], axis=0).T
        store_slabs(send.at[a], main0, main1, third)

    lane = lax.broadcasted_iota(jnp.int32, (1, 256), 1)

    @pl.loop(0, GROUPS)
    def _(g):
        for a in range(4):
            t_wait(a, g)

        @pl.when(g == GROUPS - 1)
        def _():
            s_start(0, 0)
            s_start(1, 0)

        carry = None
        for p in range(SPACE):
            window = slice(128 * p, 128 * p + 256)
            first = 16 * p
            m0 = jnp.where((lane >= first) & (lane < first + E), 1.0, 0.0).astype(BF16)
            m1 = jnp.where((lane >= first + E) & (lane < first + 2 * E), 1.0, 0.0).astype(BF16)

            def stacked(x):
                return jnp.concatenate([x * m0, x * m1], axis=0)

            q, k, c, v = (
                tin[a, :, g, :, window].astype(F32).reshape(ROWS, 256).astype(BF16) for a in range(4)
            )
            k2 = stacked(k)
            scores = dot(q, k2, NT)
            dprob = dot(c, stacked(v), NT)
            ds, low_t, ds_t = [], [], []
            for n in range(2):
                part = slice(128 * n, 128 * n + 128)
                pr = softmax(scores[:, part] * (SCALE * LOG2E) + bias[2 * p + n])
                low = pr.astype(BF16)
                d = score_grads(pr, low, dprob[:, part])
                ds.append(d)
                low_t.append(low.astype(F32).T.astype(BF16))
                ds_t.append(d.astype(F32).T.astype(BF16))
            outs = (
                dot(jnp.concatenate(ds, axis=1), k2) * SCALE,
                dot(jnp.concatenate(ds_t, axis=1), stacked(q)) * SCALE,
                dot(jnp.concatenate(low_t, axis=1), stacked(c)),
            )
            for n, out in enumerate(outs):
                left = out[:, :128] if carry is None else out[:, :128] + carry[n]
                joined[:, D * n + 128 * p:D * n + 128 * p + 128] = left.astype(BF16)
                if p == SPACE - 1:
                    joined[:, D * n + 1024:D * n + D] = out[:, 128:].astype(BF16)
            carry = [out[:, 128:] for out in outs]
        tin[0, :, g] = dot(joined[...], wq[...], NT).reshape(FRAMES, 8, D).astype(BF16)
        g_start(g)

    s_start(2, 0)
    s_start(0, 1)
    s_start(1, 1)
    for g in range(GROUPS):
        g_wait(g)
    gm_out = pltpu.make_async_copy(gm_in, gm, local_sem.at[9])
    gm_out.start()
    mid = gm_in[...].astype(F32).reshape(CLIPS, TOKENS, D)
    mid = jnp.concatenate([mid[0, :128], mid[1, :128], mid[0, 128:], mid[1, 128:]], axis=0).astype(BF16)
    cot_t = dot(wo[...], mid, NT)
    store_slabs(send.at[3], cot_t[:, :128], cot_t[:, 128:256], cot_t[:, 256:])
    s_start(3, 0)
    s_start(2, 1)
    s_start(3, 1)

    def gather(a, clip, head, dst):
        for s in range(SPACE):
            dst[:, 128 * s:128 * s + 128] = recv[a, s, clip, head]
        for m in range(SPACE // 2):
            low = recv[a, 2 * m, clip, 2].astype(F32)
            high = recv[a, 2 * m + 1, clip, 2].astype(F32)
            if head == 0:
                high = pltpu.roll(high, 64, 1)
            else:
                low = pltpu.roll(low, 64, 1)
            dst[:, 1024 + 128 * m:1152 + 128 * m] = halves(low, high).astype(BF16)

    def scatter(a, clip, head, tile, value):
        if tile < SPACE:
            send[a, tile, clip, head] = value.astype(BF16)
        elif head == 0:
            thirds[a, tile - SPACE] = value
        else:
            m = tile - SPACE
            other = thirds[a, m]
            send[a, 2 * m, clip, 2] = halves(other, pltpu.roll(value, 64, 1)).astype(BF16)
            send[a, 2 * m + 1, clip, 2] = halves(pltpu.roll(other, 64, 1), value).astype(BF16)

    @pl.loop(0, CLIPS)
    def _(clip):
        s_wait(0, clip)
        s_wait(1, clip)
        for head in range(2):
            gather(0, clip, head, q_t.at[head])
            gather(1, clip, head, k_t.at[head])
            row_n[...] = q_t[head].astype(F32).T.astype(BF16)
            for b in range(SEQ // BLOCK):
                block = slice(b * BLOCK, (b + 1) * BLOCK)
                scores = dot(row_n[block], k_t[head]) * (SCALE * LOG2E)
                probs[head, block] = softmax(scores).astype(BF16)
        s_wait(2, clip)
        s_wait(3, clip)
        for head in range(2):
            gather(2, clip, head, v_t)
            gather(3, clip, head, c_t)
            row_n[...] = c_t[...].astype(F32).T.astype(BF16)
            for b in range(SEQ // BLOCK):
                block = slice(b * BLOCK, (b + 1) * BLOCK)
                low = probs[head, block]
                ds = score_grads(low.astype(F32), low, dot(row_n[block], v_t[...]))
                to_q = dot(k_t[head], ds, NT) * SCALE
                for n in range(BLOCK // 128):
                    tile = b * (BLOCK // 128) + n
                    scatter(0, clip, head, tile, to_q[:, 128 * n:128 * n + 128])
                    if tile < SPACE:
                        b_start(0, tile, clip, head)
                to_k = dot(q_t[head, :, block], ds)
                to_v = dot(c_t[:, block], low)
                if b > 0:
                    to_k, to_v = sum_k[...] + to_k, sum_v[...] + to_v
                if b < SEQ // BLOCK - 1:
                    sum_k[...], sum_v[...] = to_k, to_v
            to_k = to_k * SCALE
            for n in range(SEQ // 128):
                scatter(1, clip, head, n, to_k[:, 128 * n:128 * n + 128])
                scatter(2, clip, head, n, to_v[:, 128 * n:128 * n + 128])
            b_start_all(1, clip, head)
            b_start_all(2, clip, head)
            if head == 1:
                for a in range(3):
                    b_start_all(a, clip, 2)

    outs = []
    for clip in range(CLIPS):
        own = [
            pltpu.make_async_copy(send.at[a, ms, clip], back.at[a, ms, clip], local_sem.at[a])
            for a in range(3)
        ]
        for copy in own:
            copy.start()
        for copy in own:
            copy.wait()
        for a in range(3):
            b_wait(a, clip, 0)
            main = back[a, :, clip, 0:2].astype(F32).reshape(D, 128)
            sin[a, clip, 0:128, :] = main.T.astype(BF16)
        for a, out in enumerate((gq, gk, gv)):
            b_wait(a, clip, 1)
            third = back[a, :, clip, 2].astype(F32)
            odd = pltpu.roll(third.reshape(SPACE * E, 128), 64, 1).reshape(SPACE, 1, E, 128)
            third = jnp.concatenate([third.reshape(SPACE, 1, E, 128), odd], axis=1).reshape(D, 128)
            sin[a, clip, 128:192, :] = third.T[0:64].astype(BF16)
            outs.append(pltpu.make_async_copy(sin.at[a, clip], out.at[clip], out_sem.at[a, clip]))
            outs[-1].start()
    gm_out.wait()
    for copy in outs:
        copy.wait()


def copy_kernel(a, b, c, d, a_out, b_out, c_out, d_out, held, in_sem, out_sem):
    reads, writes = [], []
    for n, (src, dst) in enumerate(((a, a_out), (b, b_out), (c, c_out), (d, d_out))):
        for half in range(2):
            rows = slice(192 * half, 192 * half + 192)
            reads.append(pltpu.make_async_copy(src.at[rows], held.at[n, rows], in_sem.at[n, half]))
            writes.append(pltpu.make_async_copy(held.at[n, rows], dst.at[rows], out_sem.at[n, half]))
    for copy in reads:
        copy.start()
    for read, write in zip(reads, writes):
        read.wait()
        write.start()
    for copy in writes:
        copy.wait()


def on_device(
    q_spatial, k_spatial, v_spatial, q_temporal, k_temporal, v_temporal, grad_out,
    inpaint_mask, frame_order, rel_bias, w_qkv, w_out,
):
    chunks = (FRAMES, GROUPS, 8, D)
    shape = (CLIPS, TOKENS, D)
    slabs = (SPACE, CLIPS, 3, E, 128)
    hbm = pl.BlockSpec(memory_space=pl.ANY)
    dma = pltpu.SemaphoreType.DMA
    results = pl.pallas_call(
        kernel,
        out_shape=(jax.ShapeDtypeStruct(shape, BF16),) * 3 + (jax.ShapeDtypeStruct(chunks, BF16),),
        in_specs=[hbm] * 12,
        out_specs=(hbm,) * 4,
        scratch_shapes=[
            pltpu.VMEM((CLIPS, 1, TOKENS), jnp.int32),
            pltpu.SMEM((FRAMES,), jnp.int32),
            pltpu.SMEM((HEADS, 2 * FRAMES - 1), F32),
            pltpu.VMEM(chunks, BF16),
            pltpu.VMEM((4,) + chunks, BF16),
            pltpu.VMEM((HEADS, ROWS, ROWS), F32),
            pltpu.VMEM((ROWS, 3 * D), BF16),
            pltpu.VMEM(chunks, BF16),
            pltpu.VMEM((3,) + shape, BF16),
            pltpu.VMEM((4,) + slabs, BF16),
            pltpu.VMEM((4,) + slabs, BF16),
            pltpu.VMEM((3,) + slabs, BF16),
            pltpu.VMEM((D, 3 * D), BF16),
            pltpu.VMEM((D, D), BF16),
            pltpu.VMEM((2, SEQ, SEQ), BF16),
            *(pltpu.VMEM((2, E, SEQ), BF16) for _ in range(2)),
            *(pltpu.VMEM((E, SEQ), BF16) for _ in range(2)),
            pltpu.VMEM((SEQ, E), BF16),
            *(pltpu.VMEM((E, SEQ), F32) for _ in range(2)),
            pltpu.VMEM((3, 4, E, 128), F32),
            dma((4, GROUPS)), dma((4, GROUPS)), dma((GROUPS,)), dma((GROUPS,)),
            dma((4, CLIPS)), dma((4, CLIPS)), dma((3, CLIPS, 2)), dma((3, CLIPS, 2)),
            dma((10,)), dma((9, GROUPS)), dma((3, CLIPS)),
        ],
        compiler_params=pltpu.CompilerParams(
            collective_id=0, has_side_effects=True, vmem_limit_bytes=63 * 2**20
        ),
    )(
        q_temporal.reshape(chunks), k_temporal.reshape(chunks), v_temporal.reshape(chunks),
        grad_out.reshape(chunks), inpaint_mask, frame_order, rel_bias,
        q_spatial.reshape(shape), k_spatial.reshape(shape), v_spatial.reshape(shape), w_qkv, w_out,
    )
    flat = (CLIPS * TOKENS, D)
    results = pl.pallas_call(
        copy_kernel,
        out_shape=(jax.ShapeDtypeStruct(flat, BF16),) * 4,
        in_specs=[hbm] * 4,
        out_specs=(hbm,) * 4,
        scratch_shapes=[pltpu.VMEM((4,) + flat, BF16), dma((4, 2)), dma((4, 2))],
    )(*(r.reshape(flat) for r in results))
    return tuple(r.reshape(CLIPS, 1, TOKENS, D) for r in results)


def solution(mesh):
    split = P(None, "frame", "space", None)
    in_specs = (split,) * 7 + (P(None, "frame", "space"), P(), P(), P(), P())
    return jax.shard_map(
        on_device, mesh=mesh, in_specs=in_specs, out_specs=(split,) * 4, check_vma=False
    )
```

```python
import jax
import jax.numpy as jnp
from jax import lax
from jax.experimental import pallas as pl
from jax.experimental.pallas import tpu as pltpu
from jax.sharding import PartitionSpec as P

HEADS = 16
E = 72
D = 1152
CLIPS = 2
FRAMES = 16
TOKENS = 192
SEQ = 1536
SPACE = 8
GROUPS = 3
ROWS = 128
BLOCK = 512
SCALE = E ** (-0.5)
LOG2E = 1.4426950408889634
MESH = pl.DeviceIdType.MESH
FRAME_ORDER = (12, 2, 10, 14, 6, 4, 8, 11, 3, 13, 5, 9, 7, 15, 1)
NN = (((1,), (0,)), ((), ()))
NT = (((1,), (1,)), ((), ()))
F32 = jnp.float32
BF16 = jnp.bfloat16


def dot(a, b, dims=NN):
    return lax.dot_general(a, b, dims, preferred_element_type=F32)


def softmax(scores):
    weights = jnp.exp2(scores - jnp.max(scores, axis=1, keepdims=True))
    return weights * (1.0 / jnp.sum(weights, axis=1, keepdims=True))


def score_grads(probs, probs_low, dprob):
    delta = jnp.sum(probs_low.astype(F32) * dprob, axis=1, keepdims=True)
    return (probs * (dprob - delta)).astype(BF16)


def halves(low, high):
    lane = lax.broadcasted_iota(jnp.int32, low.shape, 1)
    return jnp.where(lane < 64, low, high)


def store_slabs(dst, main0, main1, third):
    for clip, main in enumerate((main0, main1)):
        by_head = main.reshape(SPACE, 2, E, 128)
        dst[:, clip, 0] = by_head[:, 0].astype(BF16)
        dst[:, clip, 1] = by_head[:, 1].astype(BF16)
    by_head = third.reshape(SPACE, 2, E, 128)
    even = by_head[:, 0].reshape(SPACE * E, 128)
    odd = by_head[:, 1].reshape(SPACE * E, 128)
    dst[:, 0, 2] = halves(even, pltpu.roll(odd, 64, 1)).reshape(SPACE, E, 128).astype(BF16)
    dst[:, 1, 2] = halves(pltpu.roll(even, 64, 1), odd).reshape(SPACE, E, 128).astype(BF16)


def kernel(
    qt, kt, vt, go, mask_in, order_in, bias_in, qs, ks, vs, wqkv, wout,
    gq, gk, gv, gm,
    mask, order, rel_bias, cot, tin, bias, joined, gm_in, sin, send, recv, back, wq, wo,
    probs, q_t, k_t, v_t, c_t, row_n, sum_k, sum_v, thirds,
    t_send_sem, t_recv_sem, g_send_sem, g_recv_sem, s_send_sem, s_recv_sem, b_send_sem, b_recv_sem,
    local_sem, own_sem, out_sem,
):
    mf, ms = lax.axis_index("frame"), lax.axis_index("space")
    barrier = pltpu.get_barrier_semaphore()

    @pl.loop(1, FRAMES)
    def _(i):
        pl.semaphore_signal(barrier, inc=1, device_id=(lax.rem(mf + i, FRAMES), ms), device_id_type=MESH)

    @pl.loop(1, SPACE)
    def _(i):
        pl.semaphore_signal(barrier, inc=1, device_id=(mf, lax.rem(ms + i, SPACE)), device_id_type=MESH)

    loads = [
        pltpu.make_async_copy(src, dst, local_sem.at[n])
        for n, (src, dst) in enumerate(
            (
                (go, cot), (mask_in, mask), (order_in, order), (bias_in, rel_bias),
                (qs, sin.at[0]), (ks, sin.at[1]), (vs, sin.at[2]), (wqkv, wq), (wout, wo),
            )
        )
    ]
    for copy in loads[:4]:
        copy.start()
    pl.semaphore_wait(barrier, FRAMES + SPACE - 2)

    sources = (qt, kt, cot, vt)

    def t_start(a, g):
        for i in FRAME_ORDER:
            peer = lax.rem(mf + i, FRAMES)
            pltpu.make_async_remote_copy(
                src_ref=sources[a].at[peer, g], dst_ref=tin.at[a, mf, g],
                send_sem=t_send_sem.at[a, g], recv_sem=t_recv_sem.at[a, g],
                device_id=(peer, ms), device_id_type=MESH,
            ).start()
        pltpu.make_async_copy(sources[a].at[mf, g], tin.at[a, mf, g], own_sem.at[a, g]).start()

    def t_wait(a, g):
        some = tin.at[a, 0:FRAMES - 1, g]
        sems = (t_send_sem.at[a, g], t_recv_sem.at[a, g])
        pltpu.make_async_copy(sources[a].at[mf, g], tin.at[a, mf, g], own_sem.at[a, g]).wait()
        for sem in sems:
            pltpu.make_async_copy(some, some, sem).wait()

    def g_start(g):
        @pl.loop(1, FRAMES)
        def _(i):
            peer = lax.rem(mf + i, FRAMES)
            pltpu.make_async_remote_copy(
                src_ref=tin.at[0, peer, g], dst_ref=gm_in.at[mf, g],
                send_sem=g_send_sem.at[g], recv_sem=g_recv_sem.at[g],
                device_id=(peer, ms), device_id_type=MESH,
            ).start()
        pltpu.make_async_copy(tin.at[0, mf, g], gm_in.at[mf, g], own_sem.at[4, g]).start()

    def g_wait(g):
        some = gm_in.at[0:FRAMES - 1, g]
        sems = (g_send_sem.at[g], g_recv_sem.at[g])
        pltpu.make_async_copy(tin.at[0, mf, g], gm_in.at[mf, g], own_sem.at[4, g]).wait()
        for sem in sems:
            pltpu.make_async_copy(some, some, sem).wait()

    def s_start(a, clip):
        pltpu.make_async_copy(send.at[a, ms, clip], recv.at[a, ms, clip], own_sem.at[5 + a, clip]).start()
        for i in (1, 7, 3, 5, 2, 4, 6):
            peer = lax.rem(ms + i, SPACE)
            pltpu.make_async_remote_copy(
                src_ref=send.at[a, peer, clip], dst_ref=recv.at[a, ms, clip],
                send_sem=s_send_sem.at[a, clip], recv_sem=s_recv_sem.at[a, clip],
                device_id=(mf, peer), device_id_type=MESH,
            ).start()

    def s_wait(a, clip):
        some = recv.at[a, 0:SPACE - 1, clip]
        sems = (s_send_sem.at[a, clip], s_recv_sem.at[a, clip])
        pltpu.make_async_copy(send.at[a, ms, clip], recv.at[a, ms, clip], own_sem.at[5 + a, clip]).wait()
        for sem in sems:
            pltpu.make_async_copy(some, some, sem).wait()

    def b_start(a, peer, clip, slab):
        kind = slab // 2

        @pl.when(peer != ms)
        def _():
            pltpu.make_async_remote_copy(
                src_ref=send.at[a, peer, clip, slab], dst_ref=back.at[a, ms, clip, slab],
                send_sem=b_send_sem.at[a, clip, kind], recv_sem=b_recv_sem.at[a, clip, kind],
                device_id=(mf, peer), device_id_type=MESH,
            ).start()

    def b_start_all(a, clip, slab):
        kind = slab // 2
        for i in (1, 7, 3, 5, 2, 4, 6):
            peer = lax.rem(ms + i, SPACE)
            pltpu.make_async_remote_copy(
                src_ref=send.at[a, peer, clip, slab], dst_ref=back.at[a, ms, clip, slab],
                send_sem=b_send_sem.at[a, clip, kind], recv_sem=b_recv_sem.at[a, clip, kind],
                device_id=(mf, peer), device_id_type=MESH,
            ).start()

    def b_wait(a, clip, kind):
        some = back.at[a, 0:SPACE - 1, clip, 2 * kind:2 + kind]
        sems = (b_send_sem.at[a, clip, kind], b_recv_sem.at[a, clip, kind])
        for sem in sems:
            pltpu.make_async_copy(some, some, sem).wait()

    t_start(0, 0)
    t_start(1, 0)
    t_start(3, 0)
    for copy in loads[:4]:
        copy.wait()
    row = lax.broadcasted_iota(jnp.int32, (TOKENS, TOKENS), 0)
    col = lax.broadcasted_iota(jnp.int32, (TOKENS, TOKENS), 1)
    for clip in range(CLIPS):
        diagonal = jnp.where(row == col, mask[clip].astype(F32), 0.0).astype(BF16)
        masked = dot(diagonal, cot[8 * clip:8 * clip + 8].astype(F32).reshape(TOKENS, D).astype(BF16))
        cot[8 * clip:8 * clip + 8] = masked.reshape(8, GROUPS, 8, D).astype(BF16)
    t_start(2, 0)
    for g in range(1, GROUPS):
        for a in range(4):
            t_start(a, g)
    for copy in loads[4:]:
        copy.start()

    row = lax.broadcasted_iota(jnp.int32, (ROWS, ROWS), 0)
    col = lax.broadcasted_iota(jnp.int32, (ROWS, ROWS), 1)
    offset = jnp.full((ROWS, ROWS), FRAMES - 1, jnp.int32)
    for f in range(FRAMES):
        offset = offset + jnp.where((row >> 3) == f, order[f], 0) - jnp.where((col >> 3) == f, order[f], 0)
    offset = jnp.where((row & 7) == (col & 7), offset, -1)

    @pl.loop(0, HEADS)
    def _(h):
        total = jnp.full((ROWS, ROWS), -1e30, F32)
        for o in range(2 * FRAMES - 1):
            total = jnp.where(offset == o, rel_bias[h, o] * LOG2E, total)
        bias[h] = total

    for copy in loads[4:]:
        copy.wait()

    @pl.loop(0, 3)
    def _(a):
        x = sin.at[a]
        main0 = x[0, 0:128, :].astype(F32).T
        main1 = x[1, 0:128, :].astype(F32).T
        third = jnp.concatenate([x[0, 128:192, :].astype(F32), x[1, 128:192, :].astype(F32)], axis=0).T
        store_slabs(send.at[a], main0, main1, third)

    lane = lax.broadcasted_iota(jnp.int32, (1, 256), 1)

    @pl.loop(0, GROUPS)
    def _(g):
        for a in range(4):
            t_wait(a, g)

        @pl.when(g == GROUPS - 1)
        def _():
            s_start(0, 0)
            s_start(1, 0)

        carry = None
        for p in range(SPACE):
            window = slice(128 * p, 128 * p + 256)
            first = 16 * p
            m0 = jnp.where((lane >= first) & (lane < first + E), 1.0, 0.0).astype(BF16)
            m1 = jnp.where((lane >= first + E) & (lane < first + 2 * E), 1.0, 0.0).astype(BF16)

            def stacked(x):
                return jnp.concatenate([x * m0, x * m1], axis=0)

            q, k, c, v = (
                tin[a, :, g, :, window].astype(F32).reshape(ROWS, 256).astype(BF16) for a in range(4)
            )
            k2 = stacked(k)
            scores = dot(q, k2, NT)
            dprob = dot(c, stacked(v), NT)
            ds, low_t, ds_t = [], [], []
            for n in range(2):
                part = slice(128 * n, 128 * n + 128)
                pr = softmax(scores[:, part] * (SCALE * LOG2E) + bias[2 * p + n])
                low = pr.astype(BF16)
                d = score_grads(pr, low, dprob[:, part])
                ds.append(d)
                low_t.append(low.astype(F32).T.astype(BF16))
                ds_t.append(d.astype(F32).T.astype(BF16))
            outs = (
                dot(jnp.concatenate(ds, axis=1), k2) * SCALE,
                dot(jnp.concatenate(ds_t, axis=1), stacked(q)) * SCALE,
                dot(jnp.concatenate(low_t, axis=1), stacked(c)),
            )
            for n, out in enumerate(outs):
                left = out[:, :128] if carry is None else out[:, :128] + carry[n]
                joined[:, D * n + 128 * p:D * n + 128 * p + 128] = left.astype(BF16)
                if p == SPACE - 1:
                    joined[:, D * n + 1024:D * n + D] = out[:, 128:].astype(BF16)
            carry = [out[:, 128:] for out in outs]
        tin[0, :, g] = dot(joined[...], wq[...], NT).reshape(FRAMES, 8, D).astype(BF16)
        g_start(g)

    s_start(2, 0)
    s_start(0, 1)
    s_start(1, 1)
    for g in range(GROUPS):
        g_wait(g)
    gm_out = pltpu.make_async_copy(gm_in, gm, local_sem.at[9])
    gm_out.start()
    mid = gm_in[...].astype(F32).reshape(CLIPS, TOKENS, D)
    mid = jnp.concatenate([mid[0, :128], mid[1, :128], mid[0, 128:], mid[1, 128:]], axis=0).astype(BF16)
    cot_t = dot(wo[...], mid, NT)
    store_slabs(send.at[3], cot_t[:, :128], cot_t[:, 128:256], cot_t[:, 256:])
    s_start(3, 0)
    s_start(2, 1)
    s_start(3, 1)

    def gather(a, clip, head, dst):
        for s in range(SPACE):
            dst[:, 128 * s:128 * s + 128] = recv[a, s, clip, head]
        for m in range(SPACE // 2):
            low = recv[a, 2 * m, clip, 2].astype(F32)
            high = recv[a, 2 * m + 1, clip, 2].astype(F32)
            if head == 0:
                high = pltpu.roll(high, 64, 1)
            else:
                low = pltpu.roll(low, 64, 1)
            dst[:, 1024 + 128 * m:1152 + 128 * m] = halves(low, high).astype(BF16)

    def scatter(a, clip, head, tile, value):
        if tile < SPACE:
            send[a, tile, clip, head] = value.astype(BF16)
        elif head == 0:
            thirds[a, tile - SPACE] = value
        else:
            m = tile - SPACE
            other = thirds[a, m]
            send[a, 2 * m, clip, 2] = halves(other, pltpu.roll(value, 64, 1)).astype(BF16)
            send[a, 2 * m + 1, clip, 2] = halves(pltpu.roll(other, 64, 1), value).astype(BF16)

    @pl.loop(0, CLIPS)
    def _(clip):
        s_wait(0, clip)
        s_wait(1, clip)
        for head in range(2):
            gather(0, clip, head, q_t.at[head])
            gather(1, clip, head, k_t.at[head])
            row_n[...] = q_t[head].astype(F32).T.astype(BF16)
            for b in range(SEQ // BLOCK):
                block = slice(b * BLOCK, (b + 1) * BLOCK)
                scores = dot(row_n[block], k_t[head]) * (SCALE * LOG2E)
                probs[head, block] = softmax(scores).astype(BF16)
        s_wait(2, clip)
        s_wait(3, clip)
        for head in range(2):
            gather(2, clip, head, v_t)
            gather(3, clip, head, c_t)
            row_n[...] = c_t[...].astype(F32).T.astype(BF16)
            for b in range(SEQ // BLOCK):
                block = slice(b * BLOCK, (b + 1) * BLOCK)
                low = probs[head, block]
                ds = score_grads(low.astype(F32), low, dot(row_n[block], v_t[...]))
                to_q = dot(k_t[head], ds, NT) * SCALE
                for n in range(BLOCK // 128):
                    tile = b * (BLOCK // 128) + n
                    scatter(0, clip, head, tile, to_q[:, 128 * n:128 * n + 128])
                    if tile < SPACE:
                        b_start(0, tile, clip, head)
                to_k = dot(q_t[head, :, block], ds)
                to_v = dot(c_t[:, block], low)
                if b > 0:
                    to_k, to_v = sum_k[...] + to_k, sum_v[...] + to_v
                if b < SEQ // BLOCK - 1:
                    sum_k[...], sum_v[...] = to_k, to_v
            to_k = to_k * SCALE
            for n in range(SEQ // 128):
                scatter(1, clip, head, n, to_k[:, 128 * n:128 * n + 128])
                scatter(2, clip, head, n, to_v[:, 128 * n:128 * n + 128])
            b_start_all(1, clip, head)
            b_start_all(2, clip, head)
            if head == 1:
                for a in range(3):
                    b_start_all(a, clip, 2)

    outs = []
    for clip in range(CLIPS):
        own = [
            pltpu.make_async_copy(send.at[a, ms, clip], back.at[a, ms, clip], local_sem.at[a])
            for a in range(3)
        ]
        for copy in own:
            copy.start()
        for copy in own:
            copy.wait()
        for a in range(3):
            b_wait(a, clip, 0)
            main = back[a, :, clip, 0:2].astype(F32).reshape(D, 128)
            sin[a, clip, 0:128, :] = main.T.astype(BF16)
        for a, out in enumerate((gq, gk, gv)):
            b_wait(a, clip, 1)
            third = back[a, :, clip, 2].astype(F32)
            odd = pltpu.roll(third.reshape(SPACE * E, 128), 64, 1).reshape(SPACE, 1, E, 128)
            third = jnp.concatenate([third.reshape(SPACE, 1, E, 128), odd], axis=1).reshape(D, 128)
            sin[a, clip, 128:192, :] = third.T[0:64].astype(BF16)
            outs.append(pltpu.make_async_copy(sin.at[a, clip], out.at[clip], out_sem.at[a, clip]))
            outs[-1].start()
    gm_out.wait()
    for copy in outs:
        copy.wait()


def copy_kernel(a, b, c, d, a_out, b_out, c_out, d_out, held, in_sem, out_sem):
    reads, writes = [], []
    for n, (src, dst) in enumerate(((a, a_out), (b, b_out), (c, c_out), (d, d_out))):
        for half in range(2):
            rows = slice(192 * half, 192 * half + 192)
            reads.append(pltpu.make_async_copy(src.at[rows], held.at[n, rows], in_sem.at[n, half]))
            writes.append(pltpu.make_async_copy(held.at[n, rows], dst.at[rows], out_sem.at[n, half]))
    for copy in reads:
        copy.start()
    for read, write in zip(reads, writes):
        read.wait()
        write.start()
    for copy in writes:
        copy.wait()


def on_device(
    q_spatial, k_spatial, v_spatial, q_temporal, k_temporal, v_temporal, grad_out,
    inpaint_mask, frame_order, rel_bias, w_qkv, w_out,
):
    chunks = (FRAMES, GROUPS, 8, D)
    shape = (CLIPS, TOKENS, D)
    slabs = (SPACE, CLIPS, 3, E, 128)
    hbm = pl.BlockSpec(memory_space=pl.ANY)
    dma = pltpu.SemaphoreType.DMA
    results = pl.pallas_call(
        kernel,
        out_shape=(jax.ShapeDtypeStruct(shape, BF16),) * 3 + (jax.ShapeDtypeStruct(chunks, BF16),),
        in_specs=[hbm] * 12,
        out_specs=(hbm,) * 4,
        scratch_shapes=[
            pltpu.VMEM((CLIPS, 1, TOKENS), jnp.int32),
            pltpu.SMEM((FRAMES,), jnp.int32),
            pltpu.SMEM((HEADS, 2 * FRAMES - 1), F32),
            pltpu.VMEM(chunks, BF16),
            pltpu.VMEM((4,) + chunks, BF16),
            pltpu.VMEM((HEADS, ROWS, ROWS), F32),
            pltpu.VMEM((ROWS, 3 * D), BF16),
            pltpu.VMEM(chunks, BF16),
            pltpu.VMEM((3,) + shape, BF16),
            pltpu.VMEM((4,) + slabs, BF16),
            pltpu.VMEM((4,) + slabs, BF16),
            pltpu.VMEM((3,) + slabs, BF16),
            pltpu.VMEM((D, 3 * D), BF16),
            pltpu.VMEM((D, D), BF16),
            pltpu.VMEM((2, SEQ, SEQ), BF16),
            *(pltpu.VMEM((2, E, SEQ), BF16) for _ in range(2)),
            *(pltpu.VMEM((E, SEQ), BF16) for _ in range(2)),
            pltpu.VMEM((SEQ, E), BF16),
            *(pltpu.VMEM((E, SEQ), F32) for _ in range(2)),
            pltpu.VMEM((3, 4, E, 128), F32),
            dma((4, GROUPS)), dma((4, GROUPS)), dma((GROUPS,)), dma((GROUPS,)),
            dma((4, CLIPS)), dma((4, CLIPS)), dma((3, CLIPS, 2)), dma((3, CLIPS, 2)),
            dma((10,)), dma((9, GROUPS)), dma((3, CLIPS)),
        ],
        compiler_params=pltpu.CompilerParams(
            collective_id=0, has_side_effects=True, vmem_limit_bytes=63 * 2**20
        ),
    )(
        q_temporal.reshape(chunks), k_temporal.reshape(chunks), v_temporal.reshape(chunks),
        grad_out.reshape(chunks), inpaint_mask, frame_order, rel_bias,
        q_spatial.reshape(shape), k_spatial.reshape(shape), v_spatial.reshape(shape), w_qkv, w_out,
    )
    flat = (CLIPS * TOKENS, D)
    results = pl.pallas_call(
        copy_kernel,
        out_shape=(jax.ShapeDtypeStruct(flat, BF16),) * 4,
        in_specs=[hbm] * 4,
        out_specs=(hbm,) * 4,
        scratch_shapes=[pltpu.VMEM((4,) + flat, BF16), dma((4, 2)), dma((4, 2))],
    )(*(r.reshape(flat) for r in results))
    return tuple(r.reshape(CLIPS, 1, TOKENS, D) for r in results)


def solution(mesh):
    split = P(None, "frame", "space", None)
    in_specs = (split,) * 7 + (P(None, "frame", "space"), P(), P(), P(), P())
    return jax.shard_map(
        on_device, mesh=mesh, in_specs=in_specs, out_specs=(split,) * 4, check_vma=False
    )
```
